128 devices in a mesh: gx: 16 (over x, z), gy: 8 (over y, core).
Axes of the slice: x: 4, y: 4, z: 4, core: 2. Of those that a mesh axis runs over, the one named last changes fastest.
Arguments:
- density: float32 [16, 8, 8, 64, 1024], P('gx', 'gy'), may hold values from -0.07 to 1.15
- moves: int32 [16, 8, 8], P('gx', 'gy'), may hold values from 0 to 1023, as said below
- cols: int32 [16, 8, 8, 16], P('gx', 'gy'), may hold values from 0 to 39, as said below
- halo_rows: int32 [16, 8, 4], P('gx', 'gy'), may hold values from 0 to 7, as said below
Outputs:
- purified: float32 [16, 8, 8, 64, 1024], P('gx', 'gy')
- occupation: float32 [4], replicated
The draws below stay inside these ranges and needn't reach their ends.
Inputs may be any that keep to these rules, and one draw needn't show every extreme that they name: moves is a permutation of the 1024 row ids. Rows leave in 8 waves: in each wave every brick sends one row to the brick beside it (periodic, among the eight around it) in that wave's direction, the waves' directions all differ, and the row lands in the slot that the receiving brick emptied in the same wave; all other rows keep their id. cols[i, j, r, 0] is r; the 16 entries of a row are distinct. `halo_rows`: the 4 entries of a brick are distinct.
All inputs are finite; a program needn't handle non-finite values.
Results may differ from the reference program's by a relative error of at most 0.0003.
Values sent between devices are 32-bit elements; how exact they have to be, the bound alone decides.
A program may use at most 192 MiB of HBM per device.

```python
import jax
import jax.numpy as jnp
import numpy as np
from jax import lax

BLOCK = 64
K = 16
ROWS_DEV = 8
HALO = 4
WAVES = 8
STEPS = 2
N_GX = 16
N_GY = 8


noise_spread = 0.015625


shift_table_x = (-1, -1, -1, 0, 0, 1, 1, 1)


shift_table_y = (-1, 0, 1, -1, 1, -1, 0, 1)


def draw_density(key, part):
    key = jax.random.fold_in(key, 11)
    noise_key, jitter_key = jax.random.split(key)
    shape = (N_GX, N_GY, ROWS_DEV, BLOCK, K * BLOCK)
    across = jnp.arange(N_GX, dtype=jnp.float32)[:, None]
    along = jnp.arange(N_GY, dtype=jnp.float32)[None, :]
    place = (across * N_GY + along) / (N_GX * N_GY - 1)
    noise = jax.random.truncated_normal(noise_key, -4.0, 4.0, shape, jnp.float32) * noise_spread
    level = 0.3 * (1.0 + 2.0 * place)
    jitter = jax.random.uniform(jitter_key, shape[:4], jnp.float32, 0.8, 1.2)
    diagonal = (jnp.arange(BLOCK)[:, None] == jnp.arange(K * BLOCK)[None, :]).astype(jnp.float32)
    occupied = level[:, :, None, None] * jitter
    return noise + occupied[..., None] * diagonal[None, None, None]


def draw_moves(key, part):
    key = jax.random.fold_in(key, 14)
    slot_key, order_key = jax.random.split(key)
    bricks = N_GX * N_GY
    orders = jax.vmap(lambda one: jax.random.permutation(one, ROWS_DEV))(jax.random.split(slot_key, bricks))
    orders = orders.reshape(N_GX, N_GY, ROWS_DEV).astype(jnp.int32)
    directions = jax.random.permutation(order_key, 8)
    table_x = jnp.array(shift_table_x, dtype=jnp.int32)
    table_y = jnp.array(shift_table_y, dtype=jnp.int32)
    across = jnp.arange(N_GX, dtype=jnp.int32)[:, None]
    along = jnp.arange(N_GY, dtype=jnp.int32)[None, :]
    slot_ids = jnp.arange(ROWS_DEV, dtype=jnp.int32)
    result = ((across * N_GY + along) * ROWS_DEV)[:, :, None] + slot_ids[None, None, :]
    for wave in range(WAVES):
        chosen = directions[wave]
        other_x = (across + table_x[chosen]) % N_GX
        other_y = (along + table_y[chosen]) % N_GY
        emptied = orders[:, :, wave]
        landing = emptied[other_x, other_y]
        target = (other_x * N_GY + other_y) * ROWS_DEV + landing
        result = jnp.where(slot_ids[None, None, :] == emptied[:, :, None], target[:, :, None], result)
    return result.astype(jnp.int32)


def draw_cols(key, part):
    key = jax.random.fold_in(key, 12)
    pool = ROWS_DEV + 8 * HALO
    count = N_GX * N_GY * ROWS_DEV
    orders = jax.vmap(lambda one: jax.random.permutation(one, pool - 1))(jax.random.split(key, count))
    orders = orders[:, :K - 1].astype(jnp.int32)
    itself = jnp.tile(jnp.arange(ROWS_DEV, dtype=jnp.int32), N_GX * N_GY)
    others = orders + (orders >= itself[:, None]).astype(jnp.int32)
    result = jnp.concatenate([itself[:, None], others], axis=1)
    return result.reshape(N_GX, N_GY, ROWS_DEV, K).astype(jnp.int32)


def draw_halo_rows(key, part):
    key = jax.random.fold_in(key, 13)
    count = N_GX * N_GY
    orders = jax.vmap(lambda one: jax.random.permutation(one, ROWS_DEV))(jax.random.split(key, count))
    return orders[:, :HALO].reshape(N_GX, N_GY, HALO).astype(jnp.int32)


def setup_inputs(seed: int = 0) -> dict:
    keys = jax.random.split(jax.random.key(seed), 5)
    density = draw_density(jax.random.fold_in(keys[4], 71), 0)
    moves = draw_moves(jax.random.fold_in(keys[4], 71), 0)
    cols = draw_cols(jax.random.fold_in(keys[4], 71), 0)
    halo_rows = draw_halo_rows(jax.random.fold_in(keys[4], 71), 0)
    return {"density": density, "moves": moves, "cols": cols, "halo_rows": halo_rows}


step_x = np.array([-1, -1, -1, 0, 0, 1, 1, 1])
step_y = np.array([-1, 0, 1, -1, 1, -1, 0, 1])


def global_columns(cols, halo_rows):
    across = jnp.arange(N_GX, dtype=jnp.int32)[:, None]
    along = jnp.arange(N_GY, dtype=jnp.int32)[None, :]
    firsts = (across * N_GY + along) * ROWS_DEV
    pieces = [firsts[:, :, None] + jnp.arange(ROWS_DEV, dtype=jnp.int32)[None, None, :]]
    for direction in range(8):
        other_x = (across + int(step_x[direction])) % N_GX
        other_y = (along + int(step_y[direction])) % N_GY
        listed = halo_rows[other_x, other_y].astype(jnp.int32)
        pieces.append(((other_x * N_GY + other_y) * ROWS_DEV)[:, :, None] + listed)
    table = jnp.concatenate(pieces, axis=2).astype(jnp.int32)
    picked = jnp.take_along_axis(table, cols.reshape(N_GX, N_GY, ROWS_DEV * K).astype(jnp.int32), axis=2)
    return picked.reshape(N_GX * N_GY * ROWS_DEV, K).astype(jnp.int32)


def square_on_pattern(current, columns):
    total = current.shape[0]
    blocks = current.reshape(total, BLOCK, K, BLOCK)

    def one_group(start):
        mine = lax.dynamic_slice_in_dim(blocks, start, ROWS_DEV, 0)
        my_cols = lax.dynamic_slice_in_dim(columns, start, ROWS_DEV, 0)
        far = jnp.take(blocks, my_cols, axis=0)
        far_cols = jnp.take(columns, my_cols, axis=0)
        match = (far_cols[:, :, :, None] == my_cols[:, None, None, :]).astype(jnp.float32)
        aligned = jnp.einsum('gtbuc,gtus->gtbsc', far, match, precision=lax.Precision.HIGHEST)
        return jnp.einsum('gatb,gtbsc->gasc', mine, aligned, precision=lax.Precision.HIGHEST)

    starts = jnp.arange(total // ROWS_DEV, dtype=jnp.int32) * ROWS_DEV
    return lax.map(one_group, starts).reshape(total, BLOCK, K * BLOCK)


def slot_trace(current):
    return jnp.sum(jnp.diagonal(current[:, :, :BLOCK], axis1=1, axis2=2))


def reference(density, moves, cols, halo_rows):
    total = N_GX * N_GY * ROWS_DEV
    flat = density.reshape(total, BLOCK, K * BLOCK)
    current = jnp.zeros_like(flat).at[moves.reshape(total).astype(jnp.int32)].set(flat)
    columns = global_columns(cols, halo_rows)
    scale = 1.0 / (total * BLOCK)
    sums = []
    for step in range(STEPS):
        squared = square_on_pattern(current, columns)
        sums.append(slot_trace(current) * scale)
        sums.append(slot_trace(squared) * scale)
        if step % 2 == 1:
            current = 2.0 * current - squared
        else:
            current = squared
    return current.reshape(density.shape), jnp.stack(sums).astype(jnp.float32)
```

```python
import functools

import jax
import jax.numpy as jnp
from jax import lax
from jax.experimental import pallas as pl
from jax.experimental.pallas import tpu as pltpu
from jax.sharding import PartitionSpec as P

MESH = pl.DeviceIdType.MESH
f32 = jnp.float32
bf16 = jnp.bfloat16
i32 = jnp.int32

DIRS = ((-1, -1), (-1, 0), (-1, 1), (0, -1), (0, 1), (1, -1), (1, 0), (1, 1))

ROWS = 8
SLOTS = 16
BLOCK = 64
HALO = 4
STRIP = SLOTS * BLOCK
PAIRS = SLOTS // 2
POOL = ROWS + 8 * HALO

I, Y, ZM, ZP, ZMI, ZPI, ZMY, ZPY = range(8)


def kernel(nx, ny, moves_s, rims_s, meta, dens_hbm, out_hbm, occ_s,
           dens, stage, mig, cur, halo, near, left, prod, acc, outbuf,
           info, infos, tab, tab_s, role_s, parts, sum_y, sum_x,
           local_sem, tab_sem, out_sem, mig_send, mig_recv, info_send, info_recv,
           halo_send, halo_recv, sumy_send, sumy_recv, sumx_send, sumx_recv):
    ix = lax.axis_index("gx")
    iy = lax.axis_index("gy")
    me = ix * ny + iy
    cross = 2 * lax.rem(iy, 2) - 1
    inner = -cross

    def at(dx, dy):
        return (lax.rem(ix + dx + nx, nx), lax.rem(iy + dy + ny, ny))

    load = pltpu.make_async_copy(dens_hbm.at[0, 0], dens, local_sem)
    load.start()

    barrier = pltpu.get_barrier_semaphore()
    greeted = [at(dx, dy) for dx, dy in DIRS if dx and dy]
    greeted += [at(k, 0) for k in range(1, nx)]
    greeted += [at(0, k) for k in range(1, ny)]
    for other in greeted:
        pl.semaphore_signal(barrier, inc=1, device_id=other, device_id_type=MESH)

    moves = [moves_s[0, 0, r] for r in range(ROWS)]
    rims = [rims_s[0, 0, m] for m in range(HALO)]
    row_for, slot_for = [], []
    for dx, dy in DIRS:
        ox, oy = at(dx, dy)
        brick = ox * ny + oy
        row, slot = jnp.int32(0), jnp.int32(-1)
        for r in range(ROWS):
            hit = (moves[r] >> 3) == brick
            row = jnp.where(hit, r, row)
            slot = jnp.where(hit, moves[r] & 7, slot)
        row_for.append(row)
        slot_for.append(slot)

    for m in range(HALO):
        info[pl.ds(m, 1), :] = meta[pl.ds(rims[m], 1), :]
        info[pl.ds(HALO + m, 1), :] = jnp.full((1, 128), rims[m], i32)
    for d in range(8):
        info[pl.ds(8 + d, 1), :] = jnp.full((1, 128), slot_for[d], i32)

    for role, n in ((I, 3 + (inner + 1) // 2), (Y, 3 + (cross + 1) // 2), (ZM, 1), (ZP, 6),
                    (ZMI, inner + 1), (ZPI, inner + 6), (ZMY, cross + 1), (ZPY, cross + 6)):
        role_s[role] = jnp.int32(ROWS) + HALO * n

    pl.semaphore_wait(barrier, len(greeted))

    sends = []
    for d, (dx, dy) in enumerate(DIRS):
        copy = pltpu.make_async_remote_copy(
            src_ref=info, dst_ref=infos.at[7 - d], send_sem=info_send.at[d], recv_sem=info_recv.at[7 - d],
            device_id=at(dx, dy), device_id_type=MESH)
        copy.start()
        sends.append(copy)
    load.wait()
    for d, (dx, dy) in enumerate(DIRS):
        stage[d] = dens[row_for[d]]
        copy = pltpu.make_async_remote_copy(
            src_ref=stage.at[d], dst_ref=mig.at[7 - d], send_sem=mig_send.at[d], recv_sem=mig_recv.at[7 - d],
            device_id=at(dx, dy), device_id_type=MESH)
        copy.start()
        sends.append(copy)

    flat = meta[8:16, :]
    sub = lax.broadcasted_iota(i32, (8, 128), 0)

    def matched(ids):
        found = jnp.full((8, 128), SLOTS, i32)
        for u in range(SLOTS):
            found = jnp.where(ids[:, u:u + 1] == flat, u, found)
        return found

    tab[0:8, :] = matched(meta[0:8, :])
    for group in range(POOL // 8):
        found = jnp.full((8, 128), SLOTS, i32)
        for t in range(SLOTS):
            found = jnp.where(meta[16 + t:17 + t, :] == sub + 8 * group, t, found)
        tab[POOL + 8 * group:POOL + 8 * group + 8, :] = found
    for d in range(8):
        sends[d].wait_recv()
    source = jnp.zeros((8, 128), i32)
    for n in range(8):
        dx, dy = DIRS[n]
        ids = infos[n, 0:8, :]
        pos = jnp.full((8, 128), -1, i32)
        for m in range(HALO):
            pos = jnp.where(ids == infos[n, HALO + m:HALO + m + 1, :], ROWS + HALO * n + m, pos)
        for n2, (ex, ey) in enumerate(DIRS):
            there = (dx + ex, dy + ey)
            first = ROWS + HALO * n2
            if there == (0, 0):
                for m in range(HALO):
                    pos = jnp.where(ids == first + m, rims[m], pos)
            elif there in DIRS:
                shift = HALO * (DIRS.index(there) - n2)
                pos = jnp.where((ids >= first) & (ids < first + HALO), ids + shift, pos)
        tab[ROWS + HALO * n:ROWS + HALO * n + HALO, :] = matched(pos)[:HALO]
        source = jnp.where(infos[n, 8 + 7 - n:9 + 7 - n, :] == sub, n, source)
    tab[2 * POOL:2 * POOL + 8, :] = source
    to_smem = pltpu.make_async_copy(tab, tab_s, tab_sem)
    to_smem.start()

    for g in range(ROWS):
        left[g * (SLOTS + 1) + SLOTS] = jnp.zeros((BLOCK, 256), bf16)
    for k in range(4):
        prod[k * (PAIRS + 1) + PAIRS] = jnp.zeros((ROWS, BLOCK, 128), f32)
    to_smem.wait()

    for d in range(8):
        sends[8 + d].wait_recv()

    def settle(r, carry):
        home, own = jnp.int32(0), jnp.int32(0)
        for q in range(ROWS):
            hit = moves[q] == me * ROWS + r
            home = jnp.where(hit, 1, home)
            own = jnp.where(hit, q, own)
        cur[0, r] = jnp.where(home == 1, dens[own], mig[tab_s[2 * POOL + r, 0]])
        return carry

    lax.fori_loop(0, ROWS, settle, 0)

    lane = lax.broadcasted_iota(i32, (8, 128), 1)
    low = (lax.broadcasted_iota(i32, (BLOCK, 128), 1) < BLOCK)
    eye = (lax.broadcasted_iota(i32, (BLOCK, 128), 1) == lax.broadcasted_iota(i32, (BLOCK, 128), 0))
    halves = lane // BLOCK

    def trace_of(chunk):
        return jnp.sum(jnp.where(eye, chunk, 0.0), axis=0, keepdims=True)

    def split_rows(step):
        def one(g, total):
            for q in range(PAIRS):
                chunk = cur[step, g, :, 128 * q:128 * q + 128]
                turned = pltpu.roll(chunk, BLOCK, 1)
                for odd in range(2):
                    twice = jnp.where(low, turned, chunk) if odd else jnp.where(low, chunk, turned)
                    hi = twice.astype(bf16)
                    lo = (twice - hi.astype(f32)).astype(bf16)
                    left[g * (SLOTS + 1) + 2 * q + odd, :, 0:128] = hi
                    left[g * (SLOTS + 1) + 2 * q + odd, :, 128:256] = lo
            return total + trace_of(cur[step, g, :, 0:128])

        return lax.fori_loop(0, ROWS, one, jnp.zeros((1, 128), f32))

    def multiply(strip, h, k):
        hi = strip.astype(bf16)
        lo = (strip - hi.astype(f32)).astype(bf16)
        right = jnp.concatenate([hi, lo, hi, lo], axis=0)
        rows = jnp.concatenate(
            [left[g * (SLOTS + 1) + tab_s[POOL + h, g]] for g in range(ROWS)], axis=0)
        for part in range(4):
            out = jnp.dot(rows, right[:, 256 * part:256 * part + 256], preferred_element_type=f32)
            prod[k * (PAIRS + 1) + 2 * part] = out[:, 0:128].reshape(ROWS, BLOCK, 128)
            prod[k * (PAIRS + 1) + 2 * part + 1] = out[:, 128:256].reshape(ROWS, BLOCK, 128)

    def gather(hs, first):
        def one(g, carry):
            for s in range(SLOTS):
                index = g * SLOTS + s
                total = None if first else acc[index].reshape(8, 8, 128)
                for k in range(4):
                    code = tab_s[hs[k], index]
                    block = prod[k * (PAIRS + 1) + (code >> 1), g].reshape(8, 8, 128)
                    block = jnp.where((halves == (code & 1))[None], block, 0.0)
                    total = block if total is None else total + block
                acc[index] = total.reshape(BLOCK, 128)
            return carry

        lax.fori_loop(0, ROWS, one, 0)

    def own_group(step, group, first):
        def one(k, carry):
            multiply(cur[step, 4 * group + k], 4 * group + k, k)
            return carry

        lax.fori_loop(0, 4, one, 0)
        gather([4 * group + k for k in range(4)], first)

    def halo_copy(step, src, role, m, target):
        place = role * HALO + m
        return pltpu.make_async_remote_copy(
            src_ref=src, dst_ref=near.at[step, place], send_sem=halo_send.at[step, place],
            recv_sem=halo_recv.at[step, place], device_id=target, device_id_type=MESH)

    def arrival(step, role, m):
        return halo_copy(step, near.at[step, role * HALO + m], role, m, at(0, 1))

    def pass_on(step, m):
        out = []
        for role, inside, outside in ((ZM, ZMI, ZMY), (ZP, ZPI, ZPY)):
            arrival(step, role, m).wait_recv()
            src = near.at[step, role * HALO + m]
            if m < HALO - 1:
                out.append(halo_copy(step, src, outside, m, at(0, cross)))
            out.append(halo_copy(step, src, inside, m, at(0, inner)))
        for copy in out:
            copy.start()
        return out

    def pass_on_last(step):
        m = HALO - 1
        arrival(step, Y, m).wait_recv()
        src = near.at[step, Y * HALO + m]
        out = [halo_copy(step, src, ZPY, m, at(-1, 0)), halo_copy(step, src, ZMY, m, at(1, 0))]
        for copy in out:
            copy.start()
        return out

    traces = []
    for step in range(2):
        for m in range(HALO):
            halo[step, m] = cur[step, rims[m]]
        out = []
        for m in (3, 0, 1, 2):
            src = halo.at[step, m]
            out.append(halo_copy(step, src, Y, m, at(0, cross)))
        for m in range(HALO):
            src = halo.at[step, m]
            out.append(halo_copy(step, src, ZP, m, at(-1, 0)))
            out.append(halo_copy(step, src, ZM, m, at(1, 0)))
        for m in range(HALO):
            out.append(halo_copy(step, halo.at[step, m], I, m, at(0, inner)))
        for copy in out:
            copy.start()
        before = split_rows(step)
        if step == 0:
            traces.append(before)
        own_group(step, 0, True)
        out += pass_on_last(step)
        out += pass_on(step, 0)
        own_group(step, 1, False)

        def near_group(q):
            places, hs = [], []
            for k in range(4):
                role = 2 * (q // 2) + k % 2
                m = 2 * (q % 2) + k // 2
                places.append(role * HALO + m)
                hs.append(role_s[role] + m)
            for k in range(4):
                role = 2 * (q // 2) + k % 2
                m = 2 * (q % 2) + k // 2
                if role in (ZM, ZP) or (role == Y and m == HALO - 1):
                    continue
                arrival(step, role, m).wait_recv()
            base = places[0]

            def one(k, carry):
                odd = lax.rem(k, 2)
                m = k // 2
                place = base + odd * HALO + m
                h = role_s[2 * (q // 2) + odd] + 2 * (q % 2) + m
                multiply(near[step, place], h, k)
                return carry

            lax.fori_loop(0, 4, one, 0)
            gather(hs, False)

        near_group(0)
        out += pass_on(step, 1)
        near_group(1)
        out += pass_on(step, 2)
        near_group(2)
        out += pass_on(step, 3)
        for q in range(3, 8):
            near_group(q)

        def finish(g, total):
            for q in range(PAIRS):
                even = acc[g * SLOTS + 2 * q]
                odd = acc[g * SLOTS + 2 * q + 1]
                squared = jnp.where(low, even + pltpu.roll(even, BLOCK, 1), odd + pltpu.roll(odd, BLOCK, 1))
                if q == 0:
                    total = total + trace_of(squared)
                if step == 0:
                    cur[1, g, :, 128 * q:128 * q + 128] = squared
                else:
                    outbuf[g, :, 128 * q:128 * q + 128] = 2.0 * cur[1, g, :, 128 * q:128 * q + 128] - squared
            return total

        traces.append(lax.fori_loop(0, ROWS, finish, jnp.zeros((1, 128), f32)))
        sends += out

    write = pltpu.make_async_copy(outbuf, out_hbm.at[0, 0], out_sem)
    write.start()

    row = jnp.concatenate([traces[0], traces[1], traces[1], traces[2], jnp.zeros((4, 128), f32)], axis=0)

    def exchange(value, buffer, index, count, send, recv, target):
        parts[...] = value
        buffer[index] = value
        copies = []
        for k in range(1, count):
            copies.append(pltpu.make_async_remote_copy(
                src_ref=parts, dst_ref=buffer.at[index], send_sem=send.at[k], recv_sem=recv.at[k],
                device_id=target(k), device_id_type=MESH))
        for copy in copies:
            copy.start()
        for copy in copies:
            copy.wait()
        total = buffer[0]
        for k in range(1, count):
            total = total + buffer[k]
        return total

    row = exchange(row, sum_y, iy, ny, sumy_send, sumy_recv, lambda k: at(0, k))
    row = exchange(row, sum_x, ix, nx, sumx_send, sumx_recv, lambda k: at(k, 0))
    scale = 1.0 / (nx * ny * ROWS * BLOCK)
    for k in range(4):
        occ_s[k] = jnp.sum(row[k:k + 1, :]) * scale

    for d in range(16):
        sends[d].wait_send()
    for copy in sends[16:]:
        copy.wait_send()
    write.wait()


def shards(nx, ny, density, moves, cols, halo_rows):
    mine = cols.reshape(ROWS, SLOTS)
    meta = jnp.concatenate([
        jnp.pad(mine, ((0, 0), (0, 128 - SLOTS)), constant_values=-1),
        jnp.broadcast_to(mine.reshape(1, ROWS * SLOTS), (8, 128)),
        jnp.pad(mine.T, ((0, 0), (0, 128 - ROWS)), constant_values=-1),
    ], axis=0)
    dma = pltpu.SemaphoreType.DMA
    vmem = pltpu.VMEM
    smem_spec = pl.BlockSpec(memory_space=pltpu.SMEM)
    return pl.pallas_call(
        functools.partial(kernel, nx, ny),
        out_shape=(jax.ShapeDtypeStruct(density.shape, f32), jax.ShapeDtypeStruct((4,), f32)),
        in_specs=[smem_spec, smem_spec, pl.BlockSpec(memory_space=vmem), pl.BlockSpec(memory_space=pl.ANY)],
        out_specs=(pl.BlockSpec(memory_space=pl.ANY), smem_spec),
        scratch_shapes=[
            vmem((ROWS, BLOCK, STRIP), f32),
            vmem((8, BLOCK, STRIP), f32),
            vmem((8, BLOCK, STRIP), f32),
            vmem((2, ROWS, BLOCK, STRIP), f32),
            vmem((2, HALO, BLOCK, STRIP), f32),
            vmem((2, 8 * HALO, BLOCK, STRIP), f32),
            vmem((ROWS * (SLOTS + 1), BLOCK, 256), bf16),
            vmem((4 * (PAIRS + 1), ROWS, BLOCK, 128), f32),
            vmem((ROWS * SLOTS, BLOCK, 128), f32),
            vmem((ROWS, BLOCK, STRIP), f32),
            vmem((16, 128), i32),
            vmem((8, 16, 128), i32),
            vmem((2 * POOL + 8, 128), i32),
            pltpu.SMEM((2 * POOL + 8, 128), i32),
            pltpu.SMEM((8,), i32),
            vmem((8, 128), f32),
            vmem((ny, 8, 128), f32),
            vmem((nx, 8, 128), f32),
            dma, dma, dma,
            dma((8,)), dma((8,)), dma((8,)), dma((8,)),
            dma((2, 8 * HALO)), dma((2, 8 * HALO)),
            dma((ny,)), dma((ny,)), dma((nx,)), dma((nx,)),
        ],
        compiler_params=pltpu.CompilerParams(
            collective_id=0, has_side_effects=True, vmem_limit_bytes=60 * 1024 * 1024),
    )(moves, halo_rows, meta, density)


def solution(mesh):
    nx, ny = mesh.shape["gx"], mesh.shape["gy"]
    in_specs = (
        P("gx", "gy", None, None, None),
        P("gx", "gy", None),
        P("gx", "gy", None, None),
        P("gx", "gy", None),
    )
    out_specs = (P("gx", "gy", None, None, None), P())
    return jax.shard_map(functools.partial(shards, nx, ny), mesh=mesh, in_specs=in_specs, out_specs=out_specs,
                         check_vma=False)
```

```python
import functools

import jax
import jax.numpy as jnp
from jax import lax
from jax.experimental import pallas as pl
from jax.experimental.pallas import tpu as pltpu
from jax.sharding import PartitionSpec as P

MESH = pl.DeviceIdType.MESH
f32 = jnp.float32
bf16 = jnp.bfloat16
i32 = jnp.int32

DIRS = ((-1, -1), (-1, 0), (-1, 1), (0, -1), (0, 1), (1, -1), (1, 0), (1, 1))

ROWS = 8
SLOTS = 16
BLOCK = 64
HALO = 4
STRIP = SLOTS * BLOCK
PAIRS = SLOTS // 2
POOL = ROWS + 8 * HALO

PLACE = tuple(4 * (s // 4) + (0, 2, 1, 3)[s % 4] for s in range(SLOTS))

I, Y, ZM, ZP, ZMI, ZPI, ZMY, ZPY = range(8)


def kernel(nx, ny, moves_s, rims_s, cols, dens_hbm, out_hbm, occ_s,
           dens, stage, mig, cur, halo, near, left, prod, acc,
           info, infos, tab, tab_s, role_s, parts, sum_y, sum_x,
           local_sem, tab_sem, out_sem, mig_send, mig_recv, info_send, info_recv,
           halo_send, halo_recv, sumy_send, sumy_recv, sumx_send, sumx_recv):
    ix = lax.axis_index("gx")
    iy = lax.axis_index("gy")
    me = ix * ny + iy
    cross = 2 * lax.rem(iy, 2) - 1
    inner = -cross

    def at(dx, dy):
        return (lax.rem(ix + dx + nx, nx), lax.rem(iy + dy + ny, ny))

    load = pltpu.make_async_copy(dens_hbm.at[0, 0], dens, local_sem)
    load.start()

    barrier = pltpu.get_barrier_semaphore()
    greeted = [at(dx, dy) for dx, dy in DIRS if dx and dy]
    greeted += [at(k, 0) for k in range(1, nx)]
    greeted += [at(0, k) for k in range(1, ny)]
    for other in greeted:
        pl.semaphore_signal(barrier, inc=1, device_id=other, device_id_type=MESH)

    moves = [moves_s[0, 0, r] for r in range(ROWS)]
    rims = [rims_s[0, 0, m] for m in range(HALO)]
    row_for, slot_for = [], []
    for dx, dy in DIRS:
        ox, oy = at(dx, dy)
        brick = ox * ny + oy
        row, slot = jnp.int32(0), jnp.int32(-1)
        for r in range(ROWS):
            hit = (moves[r] >> 3) == brick
            row = jnp.where(hit, r, row)
            slot = jnp.where(hit, moves[r] & 7, slot)
        row_for.append(row)
        slot_for.append(slot)

    info[...] = jnp.full((16, 128), -1, i32)
    for m in range(HALO):
        info[pl.ds(m, 1), 0:SLOTS] = cols[0, 0, pl.ds(rims[m], 1), :]
        info[pl.ds(HALO + m, 1), :] = jnp.full((1, 128), rims[m], i32)
    for d in range(8):
        info[pl.ds(8 + d, 1), :] = jnp.full((1, 128), slot_for[d], i32)

    for role, n in ((I, 3 + (inner + 1) // 2), (Y, 3 + (cross + 1) // 2), (ZM, 1), (ZP, 6),
                    (ZMI, inner + 1), (ZPI, inner + 6), (ZMY, cross + 1), (ZPY, cross + 6)):
        role_s[role] = jnp.int32(ROWS) + HALO * n

    pl.semaphore_wait(barrier, len(greeted))

    def turn_row(src, dst):
        for q in range(4):
            tile = jnp.concatenate([src[:, 256 * q:256 * q + 128], src[:, 256 * q + 128:256 * q + 256]], axis=0)
            turned = jnp.transpose(tile)
            dst[:, 256 * q:256 * q + 128] = turned[0:BLOCK]
            dst[:, 256 * q + 128:256 * q + 256] = turned[BLOCK:]

    sends = []
    for d, (dx, dy) in enumerate(DIRS):
        copy = pltpu.make_async_remote_copy(
            src_ref=info, dst_ref=infos.at[7 - d], send_sem=info_send.at[d], recv_sem=info_recv.at[7 - d],
            device_id=at(dx, dy), device_id_type=MESH)
        copy.start()
        sends.append(copy)
    load.wait()
    for d, (dx, dy) in enumerate(DIRS):
        turn_row(dens.at[row_for[d]], stage.at[d])
        copy = pltpu.make_async_remote_copy(
            src_ref=stage.at[d], dst_ref=mig.at[7 - d], send_sem=mig_send.at[d], recv_sem=mig_recv.at[7 - d],
            device_id=at(dx, dy), device_id_type=MESH)
        copy.start()
        sends.append(copy)

    def turn(r, carry):
        turn_row(dens.at[r], dens.at[r])
        return carry

    lax.fori_loop(0, ROWS, turn, 0)

    flat = jnp.broadcast_to(
        jnp.concatenate([cols[0, 0, g:g + 1, :] for g in range(ROWS)], axis=1), (8, 128))
    slot = lax.rem(lax.broadcasted_iota(i32, (8, 128), 1), SLOTS)
    middle = lax.rem(slot, 4)
    place = slot + jnp.where(middle == 1, 1, 0) - jnp.where(middle == 2, 1, 0)
    sub = lax.broadcasted_iota(i32, (8, 128), 0)

    def matched(ids):
        found = jnp.full((8, 128), SLOTS, i32)
        for u in range(SLOTS):
            found = jnp.where(ids[:, u:u + 1] == flat, PLACE[u], found)
        return found

    tab[0:8, :] = matched(cols[0, 0])
    for group in range(POOL // 8):
        found = jnp.where(flat == sub + 8 * group, place - SLOTS, 0)
        for width in (1, 2, 4, 8):
            found = found + pltpu.roll(found, 128 - width, 1)
        found = jnp.clip(found + SLOTS, 0, SLOTS)
        tab[POOL + 8 * group:POOL + 8 * group + 8, :] = found
    for d in range(8):
        sends[d].wait_recv()
    source = jnp.zeros((8, 128), i32)
    for n in range(8):
        dx, dy = DIRS[n]
        ids = infos[n, 0:8, :]
        pos = jnp.full((8, 128), -1, i32)
        for m in range(HALO):
            pos = jnp.where(ids == infos[n, HALO + m:HALO + m + 1, :], ROWS + HALO * n + m, pos)
        for n2, (ex, ey) in enumerate(DIRS):
            there = (dx + ex, dy + ey)
            first = ROWS + HALO * n2
            if there == (0, 0):
                for m in range(HALO):
                    pos = jnp.where(ids == first + m, rims[m], pos)
            elif there in DIRS:
                shift = HALO * (DIRS.index(there) - n2)
                pos = jnp.where((ids >= first) & (ids < first + HALO), ids + shift, pos)
        tab[ROWS + HALO * n:ROWS + HALO * n + HALO, :] = matched(pos)[:HALO]
        source = jnp.where(infos[n, 8 + 7 - n:9 + 7 - n, :] == sub, n, source)
    tab[2 * POOL:2 * POOL + 8, :] = source
    to_smem = pltpu.make_async_copy(tab, tab_s, tab_sem)
    to_smem.start()

    for g in range(ROWS):
        left[g * (SLOTS + 1) + SLOTS] = jnp.zeros((128, 128), bf16)
    for k in range(4):
        prod[k * (SLOTS + 1) + SLOTS] = jnp.zeros((ROWS // 2, BLOCK, 128), f32)
    to_smem.wait()

    for d in range(8):
        sends[8 + d].wait_recv()

    def settle(r, carry):
        home, own = jnp.int32(0), jnp.int32(0)
        for q in range(ROWS):
            hit = moves[q] == me * ROWS + r
            home = jnp.where(hit, 1, home)
            own = jnp.where(hit, q, own)
        cur[0, r] = jnp.where(home == 1, dens[own], mig[tab_s[2 * POOL + r, 0]])
        return carry

    lax.fori_loop(0, ROWS, settle, 0)

    lanes = lax.broadcasted_iota(i32, (BLOCK, 128), 1)
    low = lanes < BLOCK
    low_wide = lax.broadcasted_iota(i32, (128, 128), 1) < BLOCK
    eye = lax.broadcasted_iota(i32, (BLOCK, 128), 0)
    eye_low = lanes == eye
    eye_both = lax.rem(lanes, BLOCK) == eye

    def trace_of(chunk, where):
        return jnp.sum(jnp.where(where, chunk, 0.0), axis=0, keepdims=True)

    def split_rows(step):
        def one(g, total):
            for q in range(PAIRS):
                chunk = cur[step, g, :, 128 * q:128 * q + 128]
                turned = pltpu.roll(chunk, BLOCK, 1)
                for odd in range(2):
                    twice = jnp.where(low, turned, chunk) if odd else jnp.where(low, chunk, turned)
                    hi = twice.astype(bf16)
                    lo = (twice - hi.astype(f32)).astype(bf16)
                    left[g * (SLOTS + 1) + 2 * q + odd, 0:BLOCK, :] = hi
                    left[g * (SLOTS + 1) + 2 * q + odd, BLOCK:128, :] = lo
            return total + trace_of(cur[step, g, :, 0:128], eye_low)

        return lax.fori_loop(0, ROWS, one, jnp.zeros((1, 128), f32))

    def multiply(strip, h, k):
        blocks = []
        for pair in range(ROWS // 2):
            even = left[2 * pair * (SLOTS + 1) + tab_s[POOL + h, SLOTS * 2 * pair]]
            odd = left[(2 * pair + 1) * (SLOTS + 1) + tab_s[POOL + h, SLOTS * (2 * pair + 1)]]
            blocks.append(jnp.where(low_wide, even, odd))
        weights = jnp.concatenate(blocks, axis=1)
        weights = jnp.concatenate([weights[0:BLOCK], weights[0:BLOCK], weights[BLOCK:], weights[BLOCK:]], axis=0)
        far = []
        for q in range(PAIRS):
            chunk = strip[:, 128 * q:128 * q + 128]
            hi = chunk.astype(bf16).astype(f32)
            lo = chunk - hi
            far.append(jnp.where(low, hi, pltpu.roll(lo, BLOCK, 1)).astype(bf16))
            far.append(jnp.where(low, pltpu.roll(hi, BLOCK, 1), lo).astype(bf16))
        far = jnp.concatenate(far, axis=0)
        far = jnp.concatenate([far, far], axis=1)
        for part in range(2):
            out = jnp.dot(far, weights[:, 256 * part:256 * part + 256], preferred_element_type=f32)
            for u in range(SLOTS):
                for half in range(2):
                    prod[k * (SLOTS + 1) + u, 2 * part + half] = out[
                        BLOCK * u:BLOCK * u + BLOCK, 128 * half:128 * half + 128]

    def gather(hs, fresh):
        def one(pair, carry):
            for s in range(SLOTS):
                index = pair * SLOTS + s
                total = acc[index]
                if fresh is not None:
                    total = jnp.where(fresh, 0.0, total)
                for k in range(4):
                    even = prod[k * (SLOTS + 1) + tab_s[hs[k], 2 * SLOTS * pair + s], pair]
                    odd = prod[k * (SLOTS + 1) + tab_s[hs[k], 2 * SLOTS * pair + SLOTS + s], pair]
                    total = total + jnp.where(low, even, odd)
                acc[index] = total
            return carry

        lax.fori_loop(0, ROWS // 2, one, 0)

    def group(strips, hs, fresh=None):
        for k in range(4):
            multiply(strips[k], hs[k], k)
        gather(hs, fresh)

    def halo_copy(step, src, role, m, target):
        place = role * HALO + m
        return pltpu.make_async_remote_copy(
            src_ref=src, dst_ref=near.at[step, place], send_sem=halo_send.at[step, place],
            recv_sem=halo_recv.at[step, place], device_id=target, device_id_type=MESH)

    def arrival(step, role, m):
        return halo_copy(step, near.at[step, role * HALO + m], role, m, at(0, 1))

    def passed_on(step, m):
        out = []
        for role, inside, outside in ((ZM, ZMI, ZMY), (ZP, ZPI, ZPY)):
            src = near.at[step, role * HALO + m]
            if m < HALO - 1:
                out.append(halo_copy(step, src, outside, m, at(0, cross)))
            out.append(halo_copy(step, src, inside, m, at(0, inner)))
        return out

    def passed_on_last(step):
        src = near.at[step, Y * HALO + HALO - 1]
        return [halo_copy(step, src, ZPY, HALO - 1, at(-1, 0)), halo_copy(step, src, ZMY, HALO - 1, at(1, 0))]

    def pass_on(step, m):
        arrival(step, ZM, m).wait_recv()
        arrival(step, ZP, m).wait_recv()
        for copy in passed_on(step, m):
            copy.start()

    def pass_on_last(step):
        arrival(step, Y, HALO - 1).wait_recv()
        for copy in passed_on_last(step):
            copy.start()

    traces = []
    for step in range(2):
        for m in range(HALO):
            halo[step, m] = cur[step, rims[m]]
        out = []
        for m in (3, 0, 1, 2):
            src = halo.at[step, m]
            out.append(halo_copy(step, src, Y, m, at(0, cross)))
        for m in range(HALO):
            src = halo.at[step, m]
            out.append(halo_copy(step, src, ZP, m, at(-1, 0)))
            out.append(halo_copy(step, src, ZM, m, at(1, 0)))
        for m in range(HALO):
            out.append(halo_copy(step, halo.at[step, m], I, m, at(0, inner)))
        for copy in out:
            copy.start()
        before = split_rows(step)
        if step == 0:
            traces.append(before)

        def own_group(i, carry):
            @pl.when(i == 1)
            def _():
                pass_on_last(step)
                pass_on(step, 0)

            group([cur.at[step, 4 * i + k] for k in range(4)], [4 * i + k for k in range(4)], i == 0)
            return carry

        lax.fori_loop(0, 2, own_group, 0)

        def near_group(q, carry):
            for m in range(1, HALO):
                @pl.when(q == m)
                def _():
                    pass_on(step, m)

            roles = [2 * (q // 2) + k % 2 for k in range(4)]
            ms = [2 * (q % 2) + k // 2 for k in range(4)]
            for k in range(4):
                waits = q // 2 != ZM // 2
                if k == 3:
                    waits = waits & (q != 1)

                @pl.when(waits)
                def _():
                    arrival(step, roles[k], ms[k]).wait_recv()

            group([near.at[step, roles[k] * HALO + ms[k]] for k in range(4)],
                  [role_s[roles[k]] + ms[k] for k in range(4)])
            return carry

        lax.fori_loop(0, 8, near_group, 0)

        total = jnp.zeros((1, 128), f32)
        for pair in range(ROWS // 2):
            total = total + trace_of(acc[pair * SLOTS], eye_both)
        traces.append(total)
        for m in range(HALO):
            out += passed_on(step, m)
        out += passed_on_last(step)
        sends += out

        def combine(pair, odd_row, q):
            first = acc[pair * SLOTS + PLACE[2 * q]]
            second = acc[pair * SLOTS + PLACE[2 * q + 1]]
            if odd_row:
                return jnp.where(low, pltpu.roll(first, BLOCK, 1), second)
            return jnp.where(low, first, pltpu.roll(second, BLOCK, 1))

        if step == 0:
            def finish(pair, carry):
                for odd_row in range(2):
                    for q in range(PAIRS):
                        cur[1, 2 * pair + odd_row, :, 128 * q:128 * q + 128] = combine(pair, odd_row, q)
                return carry

            lax.fori_loop(0, ROWS // 2, finish, 0)

    row = jnp.concatenate([traces[0], traces[1], traces[1], traces[2], jnp.zeros((4, 128), f32)], axis=0)

    def exchange(value, buffer, index, count, send, recv, target):
        parts[count % 3] = value
        buffer[index] = value
        copies = []
        for k in range(1, count):
            copies.append(pltpu.make_async_remote_copy(
                src_ref=parts.at[count % 3], dst_ref=buffer.at[index], send_sem=send.at[k], recv_sem=recv.at[k],
                device_id=target(k), device_id_type=MESH))
        for copy in copies:
            copy.start()
        return copies

    def exchanged(copies, buffer, count):
        for copy in copies:
            copy.wait_recv()
        total = buffer[0]
        for k in range(1, count):
            total = total + buffer[k]
        return total

    along_y = exchange(row, sum_y, iy, ny, sumy_send, sumy_recv, lambda k: at(0, k))

    def last(pair, carry):
        for odd_row in range(2):
            g = 2 * pair + odd_row
            for q in range(4):
                tiles = []
                for half in range(2):
                    chunk = cur[1, g, :, 256 * q + 128 * half:256 * q + 128 * half + 128]
                    tiles.append(2.0 * chunk - combine(pair, odd_row, 2 * q + half))
                turned = jnp.transpose(jnp.concatenate(tiles, axis=0))
                dens[g, :, 256 * q:256 * q + 128] = turned[0:BLOCK]
                dens[g, :, 256 * q + 128:256 * q + 256] = turned[BLOCK:]
        return carry

    lax.fori_loop(0, ROWS // 2, last, 0)
    write = pltpu.make_async_copy(dens, out_hbm.at[0, 0], out_sem)
    write.start()

    row = exchanged(along_y, sum_y, ny)
    along_x = exchange(row, sum_x, ix, nx, sumx_send, sumx_recv, lambda k: at(k, 0))
    row = exchanged(along_x, sum_x, nx)
    scale = 1.0 / (nx * ny * ROWS * BLOCK)
    for k in range(4):
        occ_s[k] = jnp.sum(row[k:k + 1, :]) * scale

    for d in range(16):
        sends[d].wait_send()
    for copy in sends[16:] + along_y + along_x:
        copy.wait_send()
    write.wait()


def shards(nx, ny, density, moves, cols, halo_rows):
    dma = pltpu.SemaphoreType.DMA
    vmem = pltpu.VMEM
    smem_spec = pl.BlockSpec(memory_space=pltpu.SMEM)
    return pl.pallas_call(
        functools.partial(kernel, nx, ny),
        out_shape=(jax.ShapeDtypeStruct(density.shape, f32), jax.ShapeDtypeStruct((4,), f32)),
        in_specs=[smem_spec, smem_spec, pl.BlockSpec(memory_space=vmem), pl.BlockSpec(memory_space=pl.ANY)],
        out_specs=(pl.BlockSpec(memory_space=pl.ANY), smem_spec),
        scratch_shapes=[
            vmem((ROWS, BLOCK, STRIP), f32),
            vmem((8, BLOCK, STRIP), f32),
            vmem((8, BLOCK, STRIP), f32),
            vmem((2, ROWS, BLOCK, STRIP), f32),
            vmem((2, HALO, BLOCK, STRIP), f32),
            vmem((2, 8 * HALO, BLOCK, STRIP), f32),
            vmem((ROWS * (SLOTS + 1), 128, 128), bf16),
            vmem((4 * (SLOTS + 1), ROWS // 2, BLOCK, 128), f32),
            vmem((ROWS // 2 * SLOTS, BLOCK, 128), f32),
            vmem((16, 128), i32),
            vmem((8, 16, 128), i32),
            vmem((2 * POOL + 8, 128), i32),
            pltpu.SMEM((2 * POOL + 8, 128), i32),
            pltpu.SMEM((8,), i32),
            vmem((3, 8, 128), f32),
            vmem((ny, 8, 128), f32),
            vmem((nx, 8, 128), f32),
            dma, dma, dma,
            dma((8,)), dma((8,)), dma((8,)), dma((8,)),
            dma((2, 8 * HALO)), dma((2, 8 * HALO)),
            dma((ny,)), dma((ny,)), dma((nx,)), dma((nx,)),
        ],
        compiler_params=pltpu.CompilerParams(
            collective_id=0, has_side_effects=True, vmem_limit_bytes=60 * 1024 * 1024),
    )(moves, halo_rows, cols, density)


def solution(mesh):
    nx, ny = mesh.shape["gx"], mesh.shape["gy"]
    in_specs = (
        P("gx", "gy", None, None, None),
        P("gx", "gy", None),
        P("gx", "gy", None, None),
        P("gx", "gy", None),
    )
    out_specs = (P("gx", "gy", None, None, None), P())
    return jax.shard_map(functools.partial(shards, nx, ny), mesh=mesh, in_specs=in_specs, out_specs=out_specs,
                         check_vma=False)
```

```python
import functools

import jax
import jax.numpy as jnp
from jax import lax
from jax.experimental import pallas as pl
from jax.experimental.pallas import tpu as pltpu
from jax.sharding import PartitionSpec as P

MESH = pl.DeviceIdType.MESH
f32 = jnp.float32
bf16 = jnp.bfloat16
i32 = jnp.int32

DIRS = ((-1, -1), (-1, 0), (-1, 1), (0, -1), (0, 1), (1, -1), (1, 0), (1, 1))

ROWS = 8
SLOTS = 16
BLOCK = 64
HALO = 4
STRIP = SLOTS * BLOCK
PAIRS = SLOTS // 2
POOL = ROWS + 8 * HALO

PLACE = tuple(4 * (s // 4) + (0, 2, 1, 3)[s % 4] for s in range(SLOTS))

I, Y, ZM, ZP, ZMI, ZPI, ZMY, ZPY = range(8)

ARRIVING = (
    ((I, 0), (I, 1), (I, 2), (I, 3)),
    ((Y, 3), (Y, 0), (ZM, 0), (ZP, 0)),
    ((ZMI, 0), (ZPI, 0), (Y, 1), (Y, 2)),
    ((ZM, 1), (ZP, 1), (ZMI, 1), (ZPI, 1)),
    ((ZM, 2), (ZP, 2), (ZMY, 0), (ZPY, 0)),
    ((ZMI, 2), (ZPI, 2), (ZM, 3), (ZP, 3)),
    ((ZMI, 3), (ZPI, 3), (ZMY, 1), (ZPY, 1)),
    ((ZMY, 2), (ZPY, 2), (ZMY, 3), (ZPY, 3)),
)
PASS_BEFORE = (0, 2, 4, 5)


def kernel(nx, ny, moves_s, rims_s, cols, dens_hbm, out_hbm, occ_s,
           dens, stage, mig, cur, halo, near, left, prod, acc,
           info, infos, tab, tab_s, role_s, parts, sum_y, sum_x,
           local_sem, tab_sem, out_sem, mig_send, mig_recv, info_send, info_recv,
           halo_send, halo_recv, sumy_send, sumy_recv, sumx_send, sumx_recv):
    ix = lax.axis_index("gx")
    iy = lax.axis_index("gy")
    me = ix * ny + iy
    cross = 2 * lax.rem(iy, 2) - 1
    inner = -cross

    def at(dx, dy):
        return (lax.rem(ix + dx + nx, nx), lax.rem(iy + dy + ny, ny))

    load = pltpu.make_async_copy(dens_hbm.at[0, 0], dens, local_sem)
    load.start()

    barrier = pltpu.get_barrier_semaphore()
    greeted = [at(dx, dy) for dx, dy in DIRS if dx and dy]
    greeted += [at(k, 0) for k in range(1, nx)]
    greeted += [at(0, k) for k in range(1, ny)]
    for other in greeted:
        pl.semaphore_signal(barrier, inc=1, device_id=other, device_id_type=MESH)

    moves = [moves_s[0, 0, r] for r in range(ROWS)]
    rims = [rims_s[0, 0, m] for m in range(HALO)]
    row_for, slot_for = [], []
    for dx, dy in DIRS:
        ox, oy = at(dx, dy)
        brick = ox * ny + oy
        row, slot = jnp.int32(0), jnp.int32(-1)
        for r in range(ROWS):
            hit = (moves[r] >> 3) == brick
            row = jnp.where(hit, r, row)
            slot = jnp.where(hit, moves[r] & 7, slot)
        row_for.append(row)
        slot_for.append(slot)

    info[...] = jnp.full((16, 128), -1, i32)
    for m in range(HALO):
        info[pl.ds(m, 1), 0:SLOTS] = cols[0, 0, pl.ds(rims[m], 1), :]
        info[pl.ds(HALO + m, 1), :] = jnp.full((1, 128), rims[m], i32)
    for d in range(8):
        info[pl.ds(8 + d, 1), :] = jnp.full((1, 128), slot_for[d], i32)

    for role, n in ((I, 3 + (inner + 1) // 2), (Y, 3 + (cross + 1) // 2), (ZM, 1), (ZP, 6),
                    (ZMI, inner + 1), (ZPI, inner + 6), (ZMY, cross + 1), (ZPY, cross + 6)):
        role_s[role] = jnp.int32(ROWS) + HALO * n

    pl.semaphore_wait(barrier, len(greeted))

    def turn_row(src, dst):
        for q in range(4):
            tile = jnp.concatenate([src[:, 256 * q:256 * q + 128], src[:, 256 * q + 128:256 * q + 256]], axis=0)
            turned = jnp.transpose(tile)
            dst[:, 256 * q:256 * q + 128] = turned[0:BLOCK]
            dst[:, 256 * q + 128:256 * q + 256] = turned[BLOCK:]

    sends = []
    for d, (dx, dy) in enumerate(DIRS):
        copy = pltpu.make_async_remote_copy(
            src_ref=info, dst_ref=infos.at[7 - d], send_sem=info_send.at[d], recv_sem=info_recv.at[7 - d],
            device_id=at(dx, dy), device_id_type=MESH)
        copy.start()
        sends.append(copy)
    load.wait()
    for d, (dx, dy) in enumerate(DIRS):
        turn_row(dens.at[row_for[d]], stage.at[d])
        copy = pltpu.make_async_remote_copy(
            src_ref=stage.at[d], dst_ref=mig.at[7 - d], send_sem=mig_send.at[d], recv_sem=mig_recv.at[7 - d],
            device_id=at(dx, dy), device_id_type=MESH)
        copy.start()
        sends.append(copy)

    def turn(r, carry):
        turn_row(dens.at[r], dens.at[r])
        return carry

    lax.fori_loop(0, ROWS, turn, 0)

    flat = jnp.broadcast_to(
        jnp.concatenate([cols[0, 0, g:g + 1, :] for g in range(ROWS)], axis=1), (8, 128))
    slot = lax.rem(lax.broadcasted_iota(i32, (8, 128), 1), SLOTS)
    middle = lax.rem(slot, 4)
    place = slot + jnp.where(middle == 1, 1, 0) - jnp.where(middle == 2, 1, 0)
    sub = lax.broadcasted_iota(i32, (8, 128), 0)

    def matched(ids):
        found = jnp.full((8, 128), SLOTS, i32)
        for u in range(SLOTS):
            found = jnp.where(ids[:, u:u + 1] == flat, PLACE[u], found)
        return found

    tab[0:8, :] = matched(cols[0, 0])
    for group in range(POOL // 8):
        found = jnp.where(flat == sub + 8 * group, place - SLOTS, 0)
        for width in (1, 2, 4, 8):
            found = found + pltpu.roll(found, 128 - width, 1)
        found = jnp.clip(found + SLOTS, 0, SLOTS)
        tab[POOL + 8 * group:POOL + 8 * group + 8, :] = found
    for d in range(8):
        sends[d].wait_recv()
    source = jnp.zeros((8, 128), i32)
    for n in range(8):
        dx, dy = DIRS[n]
        ids = infos[n, 0:8, :]
        pos = jnp.full((8, 128), -1, i32)
        for m in range(HALO):
            pos = jnp.where(ids == infos[n, HALO + m:HALO + m + 1, :], ROWS + HALO * n + m, pos)
        for n2, (ex, ey) in enumerate(DIRS):
            there = (dx + ex, dy + ey)
            first = ROWS + HALO * n2
            if there == (0, 0):
                for m in range(HALO):
                    pos = jnp.where(ids == first + m, rims[m], pos)
            elif there in DIRS:
                shift = HALO * (DIRS.index(there) - n2)
                pos = jnp.where((ids >= first) & (ids < first + HALO), ids + shift, pos)
        tab[ROWS + HALO * n:ROWS + HALO * n + HALO, :] = matched(pos)[:HALO]
        source = jnp.where(infos[n, 8 + 7 - n:9 + 7 - n, :] == sub, n, source)
    tab[2 * POOL:2 * POOL + 8, :] = source
    to_smem = pltpu.make_async_copy(tab, tab_s, tab_sem)
    to_smem.start()

    for g in range(ROWS):
        left[g * (SLOTS + 1) + SLOTS] = jnp.zeros((128, 128), bf16)
    for k in range(4):
        prod[k * (SLOTS + 1) + SLOTS] = jnp.zeros((ROWS // 2, BLOCK, 128), f32)
    to_smem.wait()

    for d in range(8):
        sends[8 + d].wait_recv()

    def arrived(r):
        home, own = jnp.int32(0), jnp.int32(0)
        for q in range(ROWS):
            hit = moves[q] == me * ROWS + r
            home = jnp.where(hit, 1, home)
            own = jnp.where(hit, q, own)
        return jnp.where(home == 1, dens[own], mig[tab_s[2 * POOL + r, 0]])

    lanes = lax.broadcasted_iota(i32, (BLOCK, 128), 1)
    low = lanes < BLOCK
    low_wide = lax.broadcasted_iota(i32, (128, 128), 1) < BLOCK
    eye = lax.broadcasted_iota(i32, (BLOCK, 128), 0)
    eye_low = lanes == eye
    eye_both = lax.rem(lanes, BLOCK) == eye

    def trace_of(chunk, where):
        return jnp.sum(jnp.where(where, chunk, 0.0), axis=0, keepdims=True)

    def split_rows(step):
        def one(g, total):
            for q in range(PAIRS):
                chunk = cur[step, g, :, 128 * q:128 * q + 128]
                turned = pltpu.roll(chunk, BLOCK, 1)
                for odd in range(2):
                    twice = jnp.where(low, turned, chunk) if odd else jnp.where(low, chunk, turned)
                    hi = twice.astype(bf16)
                    lo = (twice - hi.astype(f32)).astype(bf16)
                    left[g * (SLOTS + 1) + 2 * q + odd, 0:BLOCK, :] = hi
                    left[g * (SLOTS + 1) + 2 * q + odd, BLOCK:128, :] = lo
            return total + trace_of(cur[step, g, :, 0:128], eye_low)

        return lax.fori_loop(0, ROWS, one, jnp.zeros((1, 128), f32))

    def multiply(strip, h, k):
        blocks = []
        for pair in range(ROWS // 2):
            even = left[2 * pair * (SLOTS + 1) + tab_s[POOL + h, SLOTS * 2 * pair]]
            odd = left[(2 * pair + 1) * (SLOTS + 1) + tab_s[POOL + h, SLOTS * (2 * pair + 1)]]
            blocks.append(jnp.where(low_wide, even, odd))
        weights = jnp.concatenate(blocks, axis=1)
        weights = jnp.concatenate([weights[0:BLOCK], weights[0:BLOCK], weights[BLOCK:], weights[BLOCK:]], axis=0)
        far = []
        for q in range(PAIRS):
            chunk = strip[:, 128 * q:128 * q + 128]
            hi = chunk.astype(bf16).astype(f32)
            lo = chunk - hi
            far.append(jnp.where(low, hi, pltpu.roll(lo, BLOCK, 1)).astype(bf16))
            far.append(jnp.where(low, pltpu.roll(hi, BLOCK, 1), lo).astype(bf16))
        far = jnp.concatenate(far, axis=0)
        far = jnp.concatenate([far, far], axis=1)
        for part in range(2):
            out = jnp.dot(far, weights[:, 256 * part:256 * part + 256], preferred_element_type=f32)
            for u in range(SLOTS):
                for half in range(2):
                    prod[k * (SLOTS + 1) + u, 2 * part + half] = out[
                        BLOCK * u:BLOCK * u + BLOCK, 128 * half:128 * half + 128]

    def gather(hs, fresh, slots=range(SLOTS)):
        def one(pair, carry):
            for s in slots:
                index = pair * SLOTS + s
                total = acc[index]
                if fresh is not None:
                    total = jnp.where(fresh, 0.0, total)
                for k in range(4):
                    even = prod[k * (SLOTS + 1) + tab_s[hs[k], 2 * SLOTS * pair + s], pair]
                    odd = prod[k * (SLOTS + 1) + tab_s[hs[k], 2 * SLOTS * pair + SLOTS + s], pair]
                    total = total + jnp.where(low, even, odd)
                acc[index] = total
            return carry

        lax.fori_loop(0, ROWS // 2, one, 0)

    def group(strips, hs, fresh=None):
        for k in range(4):
            multiply(strips[k], hs[k], k)
        gather(hs, fresh)

    def halo_copy(step, src, role, m, target):
        place = role * HALO + m
        return pltpu.make_async_remote_copy(
            src_ref=src, dst_ref=near.at[step, place], send_sem=halo_send.at[step, place],
            recv_sem=halo_recv.at[step, place], device_id=target, device_id_type=MESH)

    def arrival(step, role, m):
        return halo_copy(step, near.at[step, role * HALO + m], role, m, at(0, 1))

    def passed_on(step, m):
        out = []
        for role, inside, outside in ((ZM, ZMI, ZMY), (ZP, ZPI, ZPY)):
            src = near.at[step, role * HALO + m]
            if m < HALO - 1:
                out.append(halo_copy(step, src, outside, m, at(0, cross)))
            out.append(halo_copy(step, src, inside, m, at(0, inner)))
        return out

    def passed_on_last(step):
        src = near.at[step, Y * HALO + HALO - 1]
        return [halo_copy(step, src, ZPY, HALO - 1, at(-1, 0)), halo_copy(step, src, ZMY, HALO - 1, at(1, 0))]

    def pass_on(step, m):
        arrival(step, ZM, m).wait_recv()
        arrival(step, ZP, m).wait_recv()
        for copy in passed_on(step, m):
            copy.start()

    def pass_on_last(step):
        arrival(step, Y, HALO - 1).wait_recv()
        for copy in passed_on_last(step):
            copy.start()

    def chunk_of(pair, odd, q):
        first = acc[pair * SLOTS + PLACE[2 * q]]
        second = acc[pair * SLOTS + PLACE[2 * q + 1]]
        if odd:
            return jnp.where(low, pltpu.roll(first, BLOCK, 1), second)
        return jnp.where(low, first, pltpu.roll(second, BLOCK, 1))

    def combine(row, q):
        return jnp.where((row & 1) == 1, chunk_of(row >> 1, True, q), chunk_of(row >> 1, False, q))

    traces = []
    for step in range(2):
        out = []

        def send(role, m, target):
            out.append(halo_copy(step, halo.at[step, m], role, m, target))
            out[-1].start()

        for m in (3, 0, 1, 2):
            if step == 0:
                halo[step, m] = arrived(rims[m])
            else:
                for q in range(PAIRS):
                    halo[step, m, :, 128 * q:128 * q + 128] = combine(rims[m], q)
            send(Y, m, at(0, cross))
            if m < 3:
                send(ZP, m, at(-1, 0))
                send(ZM, m, at(1, 0))
        send(ZP, 3, at(-1, 0))
        send(ZM, 3, at(1, 0))
        for m in range(HALO):
            send(I, m, at(0, inner))

        def settle(r, carry):
            if step == 0:
                cur[0, r] = arrived(r)
            else:
                for odd in range(2):
                    for q in range(PAIRS):
                        cur[1, 2 * r + odd, :, 128 * q:128 * q + 128] = chunk_of(r, odd, q)
            return carry

        lax.fori_loop(0, ROWS if step == 0 else ROWS // 2, settle, 0)
        before = split_rows(step)
        if step == 0:
            traces.append(before)

        def own_group(i, carry):
            group([cur.at[step, 4 * i + k] for k in range(4)], [4 * i + k for k in range(4)], i == 0)
            return carry

        lax.fori_loop(0, 2, own_group, 0)

        def near_strips(q):
            for m in range(HALO):
                @pl.when(q == PASS_BEFORE[m])
                def _():
                    pass_on(step, m)
                    if m == 0:
                        pass_on_last(step)

            strips, hs = [], []
            for k in range(4):
                roles = sum(four[k][0] << (3 * j) for j, four in enumerate(ARRIVING))
                rows = sum(four[k][1] << (2 * j) for j, four in enumerate(ARRIVING))
                waits = sum(int(not (four[k][0] in (ZM, ZP) or four[k] == (Y, 3))) << j for j, four in enumerate(ARRIVING))
                role = (jnp.int32(roles) >> (3 * q)) & 7
                m = (jnp.int32(rows) >> (2 * q)) & 3

                @pl.when(((jnp.int32(waits) >> q) & 1) == 1)
                def _():
                    arrival(step, role, m).wait_recv()

                strips.append(near.at[step, role * HALO + m])
                hs.append(role_s[role] + m)
            return strips, hs

        def near_group(q, carry):
            group(*near_strips(q))
            return carry

        lax.fori_loop(0, 8 if step == 0 else 7, near_group, 0)
        if step == 1:
            strips, hs = near_strips(jnp.int32(7))
            for k in range(4):
                multiply(strips[k], hs[k], k)
            gather(hs, None, range(1))

        total = jnp.zeros((1, 128), f32)
        for pair in range(ROWS // 2):
            total = total + trace_of(acc[pair * SLOTS], eye_both)
        traces.append(total)
        for m in range(HALO):
            out += passed_on(step, m)
        out += passed_on_last(step)
        sends += out

    row = jnp.concatenate([traces[0], traces[1], traces[1], traces[2], jnp.zeros((4, 128), f32)], axis=0)

    def exchange(value, buffer, index, count, send, recv, target):
        parts[count % 3] = value
        buffer[index] = value
        copies = []
        for k in range(1, count):
            copies.append(pltpu.make_async_remote_copy(
                src_ref=parts.at[count % 3], dst_ref=buffer.at[index], send_sem=send.at[k], recv_sem=recv.at[k],
                device_id=target(k), device_id_type=MESH))
        for copy in copies:
            copy.start()
        return copies

    def exchanged(copies, buffer, count):
        for copy in copies:
            copy.wait_recv()
        total = buffer[0]
        for k in range(1, count):
            total = total + buffer[k]
        return total

    along_y = exchange(row, sum_y, iy, ny, sumy_send, sumy_recv, lambda k: at(0, k))

    gather(hs, None, range(1, SLOTS))

    def last(pair, carry):
        for odd_row in range(2):
            g = 2 * pair + odd_row
            for q in range(4):
                tiles = []
                for half in range(2):
                    chunk = cur[1, g, :, 256 * q + 128 * half:256 * q + 128 * half + 128]
                    tiles.append(2.0 * chunk - chunk_of(pair, odd_row, 2 * q + half))
                turned = jnp.transpose(jnp.concatenate(tiles, axis=0))
                dens[g, :, 256 * q:256 * q + 128] = turned[0:BLOCK]
                dens[g, :, 256 * q + 128:256 * q + 256] = turned[BLOCK:]
        return carry

    lax.fori_loop(0, ROWS // 2, last, 0)
    write = pltpu.make_async_copy(dens, out_hbm.at[0, 0], out_sem)
    write.start()

    row = exchanged(along_y, sum_y, ny)
    along_x = exchange(row, sum_x, ix, nx, sumx_send, sumx_recv, lambda k: at(k, 0))
    row = exchanged(along_x, sum_x, nx)
    scale = 1.0 / (nx * ny * ROWS * BLOCK)
    for k in range(4):
        occ_s[k] = jnp.sum(row[k:k + 1, :]) * scale

    for d in range(16):
        sends[d].wait_send()
    for copy in sends[16:] + along_y + along_x:
        copy.wait_send()
    write.wait()


def shards(nx, ny, density, moves, cols, halo_rows):
    dma = pltpu.SemaphoreType.DMA
    vmem = pltpu.VMEM
    smem_spec = pl.BlockSpec(memory_space=pltpu.SMEM)
    return pl.pallas_call(
        functools.partial(kernel, nx, ny),
        out_shape=(jax.ShapeDtypeStruct(density.shape, f32), jax.ShapeDtypeStruct((4,), f32)),
        in_specs=[smem_spec, smem_spec, pl.BlockSpec(memory_space=vmem), pl.BlockSpec(memory_space=pl.ANY)],
        out_specs=(pl.BlockSpec(memory_space=pl.ANY), smem_spec),
        scratch_shapes=[
            vmem((ROWS, BLOCK, STRIP), f32),
            vmem((8, BLOCK, STRIP), f32),
            vmem((8, BLOCK, STRIP), f32),
            vmem((2, ROWS, BLOCK, STRIP), f32),
            vmem((2, HALO, BLOCK, STRIP), f32),
            vmem((2, 8 * HALO, BLOCK, STRIP), f32),
            vmem((ROWS * (SLOTS + 1), 128, 128), bf16),
            vmem((4 * (SLOTS + 1), ROWS // 2, BLOCK, 128), f32),
            vmem((ROWS // 2 * SLOTS, BLOCK, 128), f32),
            vmem((16, 128), i32),
            vmem((8, 16, 128), i32),
            vmem((2 * POOL + 8, 128), i32),
            pltpu.SMEM((2 * POOL + 8, 128), i32),
            pltpu.SMEM((8,), i32),
            vmem((3, 8, 128), f32),
            vmem((ny, 8, 128), f32),
            vmem((nx, 8, 128), f32),
            dma, dma, dma,
            dma((8,)), dma((8,)), dma((8,)), dma((8,)),
            dma((2, 8 * HALO)), dma((2, 8 * HALO)),
            dma((ny,)), dma((ny,)), dma((nx,)), dma((nx,)),
        ],
        compiler_params=pltpu.CompilerParams(
            collective_id=0, has_side_effects=True, vmem_limit_bytes=60 * 1024 * 1024),
    )(moves, halo_rows, cols, density)


def solution(mesh):
    nx, ny = mesh.shape["gx"], mesh.shape["gy"]
    in_specs = (
        P("gx", "gy", None, None, None),
        P("gx", "gy", None),
        P("gx", "gy", None, None),
        P("gx", "gy", None),
    )
    out_specs = (P("gx", "gy", None, None, None), P())
    return jax.shard_map(functools.partial(shards, nx, ny), mesh=mesh, in_specs=in_specs, out_specs=out_specs,
                         check_vma=False)
```

```python
import functools

import jax
import jax.numpy as jnp
from jax import lax
from jax.experimental import pallas as pl
from jax.experimental.pallas import tpu as pltpu
from jax.sharding import PartitionSpec as P

MESH = pl.DeviceIdType.MESH
f32 = jnp.float32
bf16 = jnp.bfloat16
i32 = jnp.int32

DIRS = ((-1, -1), (-1, 0), (-1, 1), (0, -1), (0, 1), (1, -1), (1, 0), (1, 1))

ROWS = 8
SLOTS = 16
BLOCK = 64
HALO = 4
STRIP = SLOTS * BLOCK
PAIRS = SLOTS // 2
POOL = ROWS + 8 * HALO

PLACE = tuple(4 * (s // 4) + (0, 2, 1, 3)[s % 4] for s in range(SLOTS))

I, Y, ZM, ZP, ZMI, ZPI, ZMY, ZPY = range(8)

ARRIVING = (
    ((I, 0), (I, 1), (I, 2), (I, 3)),
    ((Y, 3), (Y, 0), (ZM, 0), (ZP, 0)),
    ((ZMI, 0), (ZPI, 0), (Y, 1), (Y, 2)),
    ((ZM, 1), (ZP, 1), (ZMI, 1), (ZPI, 1)),
    ((ZM, 2), (ZP, 2), (ZMY, 0), (ZPY, 0)),
    ((ZMI, 2), (ZPI, 2), (ZM, 3), (ZP, 3)),
    ((ZMI, 3), (ZPI, 3), (ZMY, 1), (ZPY, 1)),
    ((ZMY, 2), (ZPY, 2), (ZMY, 3), (ZPY, 3)),
)
PASS_BEFORE = (0, 2, 4, 5)


def kernel(nx, ny, cols, dens_hbm, result, occ_s, cols_s,
           dens, stage, mig, cur, halo, near, left, prod, acc,
           info, infos, tab, tab_s, role_s, parts, sum_y, sum_x,
           local_sem, small_sem, tab_sem, mig_send, mig_recv, info_send, info_recv,
           halo_send, halo_recv, sumy_send, sumy_recv, sumx_send, sumx_recv):
    ix = lax.axis_index("gx")
    iy = lax.axis_index("gy")
    me = ix * ny + iy
    cross = 2 * lax.rem(iy, 2) - 1
    inner = -cross

    def at(dx, dy):
        return (lax.rem(ix + dx + nx, nx), lax.rem(iy + dy + ny, ny))

    load = pltpu.make_async_copy(dens_hbm.at[0, 0], dens, local_sem)
    load.start()
    small = pltpu.make_async_copy(cols, cols_s, small_sem)
    small.start()

    barrier = pltpu.get_barrier_semaphore()
    greeted = [at(dx, dy) for dx, dy in DIRS if dx and dy]
    greeted += [at(k, 0) for k in range(1, nx)]
    greeted += [at(0, k) for k in range(1, ny)]
    for other in greeted:
        pl.semaphore_signal(barrier, inc=1, device_id=other, device_id_type=MESH)

    small.wait()

    moves = [cols_s[ROWS, r] for r in range(ROWS)]
    rims = [cols_s[ROWS + 1, m] for m in range(HALO)]
    row_for, slot_for = [], []
    for dx, dy in DIRS:
        ox, oy = at(dx, dy)
        brick = ox * ny + oy
        row, slot = jnp.int32(0), jnp.int32(-1)
        for r in range(ROWS):
            hit = (moves[r] >> 3) == brick
            row = jnp.where(hit, r, row)
            slot = jnp.where(hit, moves[r] & 7, slot)
        row_for.append(row)
        slot_for.append(slot)

    info[...] = jnp.full((16, 128), -1, i32)
    for m in range(HALO):
        info[pl.ds(m, 1), 0:SLOTS] = cols[pl.ds(rims[m], 1), :]
        info[pl.ds(HALO + m, 1), :] = jnp.full((1, 128), rims[m], i32)
    for d in range(8):
        info[pl.ds(8 + d, 1), :] = jnp.full((1, 128), slot_for[d], i32)

    for role, n in ((I, 3 + (inner + 1) // 2), (Y, 3 + (cross + 1) // 2), (ZM, 1), (ZP, 6),
                    (ZMI, inner + 1), (ZPI, inner + 6), (ZMY, cross + 1), (ZPY, cross + 6)):
        role_s[role] = jnp.int32(ROWS) + HALO * n

    def turn_row(src, dst):
        for q in range(4):
            tile = jnp.concatenate([src[:, 256 * q:256 * q + 128], src[:, 256 * q + 128:256 * q + 256]], axis=0)
            turned = jnp.transpose(tile)
            dst[:, 256 * q:256 * q + 128] = turned[0:BLOCK]
            dst[:, 256 * q + 128:256 * q + 256] = turned[BLOCK:]

    order = (1, 6, 0, 7, 2, 5, 3, 4)
    load.wait()
    for d in order[:2]:
        turn_row(dens.at[row_for[d]], stage.at[d])
    pl.semaphore_wait(barrier, len(greeted))

    sends = []
    for d, (dx, dy) in enumerate(DIRS):
        copy = pltpu.make_async_remote_copy(
            src_ref=info, dst_ref=infos.at[7 - d], send_sem=info_send.at[d], recv_sem=info_recv.at[7 - d],
            device_id=at(dx, dy), device_id_type=MESH)
        copy.start()
        sends.append(copy)
    for d in order:
        dx, dy = DIRS[d]
        if d not in order[:2]:
            turn_row(dens.at[row_for[d]], stage.at[d])
        copy = pltpu.make_async_remote_copy(
            src_ref=stage.at[d], dst_ref=mig.at[7 - d], send_sem=mig_send.at[d], recv_sem=mig_recv.at[7 - d],
            device_id=at(dx, dy), device_id_type=MESH)
        copy.start()
        sends.append(copy)

    def turn(r, carry):
        turn_row(dens.at[r], dens.at[r])
        return carry

    lax.fori_loop(0, ROWS, turn, 0)

    flat = jnp.broadcast_to(
        jnp.concatenate([cols[g:g + 1, :] for g in range(ROWS)], axis=1), (8, 128))
    slot = lax.rem(lax.broadcasted_iota(i32, (8, 128), 1), SLOTS)
    middle = lax.rem(slot, 4)
    place = slot + jnp.where(middle == 1, 1, 0) - jnp.where(middle == 2, 1, 0)
    sub = lax.broadcasted_iota(i32, (8, 128), 0)

    def matched(ids):
        found = jnp.full((8, 128), SLOTS, i32)
        for u in range(SLOTS):
            found = jnp.where(ids[:, u:u + 1] == flat, PLACE[u], found)
        return found

    tab[0:8, :] = matched(cols[0:ROWS, :])
    for group in range(POOL // 8):
        found = jnp.where(flat == sub + 8 * group, place - SLOTS, 0)
        for width in (1, 2, 4, 8):
            found = found + pltpu.roll(found, 128 - width, 1)
        found = jnp.clip(found + SLOTS, 0, SLOTS)
        tab[POOL + 8 * group:POOL + 8 * group + 8, :] = found
    for d in range(8):
        sends[d].wait_recv()
    source = jnp.zeros((8, 128), i32)
    for n in range(8):
        dx, dy = DIRS[n]
        ids = infos[n, 0:8, :]
        pos = jnp.full((8, 128), -1, i32)
        for m in range(HALO):
            pos = jnp.where(ids == infos[n, HALO + m:HALO + m + 1, :], ROWS + HALO * n + m, pos)
        for n2, (ex, ey) in enumerate(DIRS):
            there = (dx + ex, dy + ey)
            first = ROWS + HALO * n2
            if there == (0, 0):
                for m in range(HALO):
                    pos = jnp.where(ids == first + m, rims[m], pos)
            elif there in DIRS:
                shift = HALO * (DIRS.index(there) - n2)
                pos = jnp.where((ids >= first) & (ids < first + HALO), ids + shift, pos)
        tab[ROWS + HALO * n:ROWS + HALO * n + HALO, :] = matched(pos)[:HALO]
        source = jnp.where(infos[n, 8 + 7 - n:9 + 7 - n, :] == sub, n, source)
    tab[2 * POOL:2 * POOL + 8, :] = source
    to_smem = pltpu.make_async_copy(tab, tab_s, tab_sem)
    to_smem.start()

    for g in range(ROWS):
        left[g * (SLOTS + 1) + SLOTS] = jnp.zeros((128, 128), bf16)
    for k in range(4):
        prod[k * (SLOTS + 1) + SLOTS] = jnp.zeros((ROWS // 2, BLOCK, 128), f32)
    to_smem.wait()

    for d in range(8):
        sends[8 + d].wait_recv()

    def arrived(r):
        home, own = jnp.int32(0), jnp.int32(0)
        for q in range(ROWS):
            hit = moves[q] == me * ROWS + r
            home = jnp.where(hit, 1, home)
            own = jnp.where(hit, q, own)
        return jnp.where(home == 1, dens[own], mig[tab_s[2 * POOL + r, 0]])

    lanes = lax.broadcasted_iota(i32, (BLOCK, 128), 1)
    low = lanes < BLOCK
    low_wide = lax.broadcasted_iota(i32, (128, 128), 1) < BLOCK
    eye = lax.broadcasted_iota(i32, (BLOCK, 128), 0)
    eye_low = lanes == eye
    eye_both = lax.rem(lanes, BLOCK) == eye

    def trace_of(chunk, where):
        return jnp.sum(jnp.where(where, chunk, 0.0), axis=0, keepdims=True)

    def split_rows(step):
        def one(g, total):
            for q in range(PAIRS):
                chunk = cur[step, g, :, 128 * q:128 * q + 128]
                turned = pltpu.roll(chunk, BLOCK, 1)
                for odd in range(2):
                    twice = jnp.where(low, turned, chunk) if odd else jnp.where(low, chunk, turned)
                    hi = twice.astype(bf16)
                    lo = (twice - hi.astype(f32)).astype(bf16)
                    left[g * (SLOTS + 1) + 2 * q + odd, 0:BLOCK, :] = hi
                    left[g * (SLOTS + 1) + 2 * q + odd, BLOCK:128, :] = lo
            return total + trace_of(cur[step, g, :, 0:128], eye_low)

        return lax.fori_loop(0, ROWS, one, jnp.zeros((1, 128), f32))

    def multiply(strip, h, k):
        blocks = []
        for pair in range(ROWS // 2):
            even = left[2 * pair * (SLOTS + 1) + tab_s[POOL + h, SLOTS * 2 * pair]]
            odd = left[(2 * pair + 1) * (SLOTS + 1) + tab_s[POOL + h, SLOTS * (2 * pair + 1)]]
            blocks.append(jnp.where(low_wide, even, odd))
        weights = jnp.concatenate(blocks, axis=1)
        weights = jnp.concatenate([weights[0:BLOCK], weights[0:BLOCK], weights[BLOCK:], weights[BLOCK:]], axis=0)
        far = []
        for q in range(PAIRS):
            chunk = strip[:, 128 * q:128 * q + 128]
            hi = chunk.astype(bf16).astype(f32)
            lo = chunk - hi
            far.append(jnp.where(low, hi, pltpu.roll(lo, BLOCK, 1)).astype(bf16))
            far.append(jnp.where(low, pltpu.roll(hi, BLOCK, 1), lo).astype(bf16))
        far = jnp.concatenate(far, axis=0)
        far = jnp.concatenate([far, far], axis=1)
        for part in range(2):
            out = jnp.dot(far, weights[:, 256 * part:256 * part + 256], preferred_element_type=f32)
            for u in range(SLOTS):
                for half in range(2):
                    prod[k * (SLOTS + 1) + u, 2 * part + half] = out[
                        BLOCK * u:BLOCK * u + BLOCK, 128 * half:128 * half + 128]

    def gather(hs, fresh, slots=range(SLOTS)):
        def one(pair, carry):
            for s in slots:
                index = pair * SLOTS + s
                total = acc[index]
                if fresh is not None:
                    total = jnp.where(fresh, 0.0, total)
                for k in range(4):
                    even = prod[k * (SLOTS + 1) + tab_s[hs[k], 2 * SLOTS * pair + s], pair]
                    odd = prod[k * (SLOTS + 1) + tab_s[hs[k], 2 * SLOTS * pair + SLOTS + s], pair]
                    total = total + jnp.where(low, even, odd)
                acc[index] = total
            return carry

        lax.fori_loop(0, ROWS // 2, one, 0)

    def group(strips, hs, fresh=None):
        for k in range(4):
            multiply(strips[k], hs[k], k)
        gather(hs, fresh)

    def halo_copy(step, src, role, m, target):
        place = role * HALO + m
        return pltpu.make_async_remote_copy(
            src_ref=src, dst_ref=near.at[step, place], send_sem=halo_send.at[step, place],
            recv_sem=halo_recv.at[step, place], device_id=target, device_id_type=MESH)

    def arrival(step, role, m):
        return halo_copy(step, near.at[step, role * HALO + m], role, m, at(0, 1))

    def passed_on(step, m):
        out = []
        for role, inside, outside in ((ZM, ZMI, ZMY), (ZP, ZPI, ZPY)):
            src = near.at[step, role * HALO + m]
            if m < HALO - 1:
                out.append(halo_copy(step, src, outside, m, at(0, cross)))
            out.append(halo_copy(step, src, inside, m, at(0, inner)))
        return out

    def passed_on_last(step):
        src = near.at[step, Y * HALO + HALO - 1]
        return [halo_copy(step, src, ZPY, HALO - 1, at(-1, 0)), halo_copy(step, src, ZMY, HALO - 1, at(1, 0))]

    def pass_on(step, m):
        arrival(step, ZM, m).wait_recv()
        arrival(step, ZP, m).wait_recv()
        for copy in passed_on(step, m):
            copy.start()

    def pass_on_last(step):
        arrival(step, Y, HALO - 1).wait_recv()
        for copy in passed_on_last(step):
            copy.start()

    def chunk_of(pair, odd, q):
        first = acc[pair * SLOTS + PLACE[2 * q]]
        second = acc[pair * SLOTS + PLACE[2 * q + 1]]
        if odd:
            return jnp.where(low, pltpu.roll(first, BLOCK, 1), second)
        return jnp.where(low, first, pltpu.roll(second, BLOCK, 1))

    def combine(row, q):
        return jnp.where((row & 1) == 1, chunk_of(row >> 1, True, q), chunk_of(row >> 1, False, q))

    traces = []
    for step in range(2):
        out = []

        def send(role, m, target):
            out.append(halo_copy(step, halo.at[step, m], role, m, target))
            out[-1].start()

        for m in (3, 0, 1, 2):
            if step == 0:
                halo[step, m] = arrived(rims[m])
            else:
                for q in range(PAIRS):
                    halo[step, m, :, 128 * q:128 * q + 128] = combine(rims[m], q)
            send(Y, m, at(0, cross))
            if m < 3:
                send(ZP, m, at(-1, 0))
                send(ZM, m, at(1, 0))
        send(ZP, 3, at(-1, 0))
        send(ZM, 3, at(1, 0))
        for m in range(HALO):
            send(I, m, at(0, inner))

        def settle(r, carry):
            if step == 0:
                cur[0, r] = arrived(r)
            else:
                for odd in range(2):
                    for q in range(PAIRS):
                        cur[1, 2 * r + odd, :, 128 * q:128 * q + 128] = chunk_of(r, odd, q)
            return carry

        lax.fori_loop(0, ROWS if step == 0 else ROWS // 2, settle, 0)
        before = split_rows(step)
        if step == 0:
            traces.append(before)

        def own_group(i, carry):
            group([cur.at[step, 4 * i + k] for k in range(4)], [4 * i + k for k in range(4)], i == 0)
            return carry

        lax.fori_loop(0, 2, own_group, 0)

        def near_strips(q):
            for m in range(HALO):
                @pl.when(q == PASS_BEFORE[m])
                def _():
                    pass_on(step, m)
                    if m == 0:
                        pass_on_last(step)

            strips, hs = [], []
            for k in range(4):
                roles = sum(four[k][0] << (3 * j) for j, four in enumerate(ARRIVING))
                rows = sum(four[k][1] << (2 * j) for j, four in enumerate(ARRIVING))
                waits = sum(int(not (four[k][0] in (ZM, ZP) or four[k] == (Y, 3))) << j for j, four in enumerate(ARRIVING))
                role = (jnp.int32(roles) >> (3 * q)) & 7
                m = (jnp.int32(rows) >> (2 * q)) & 3

                @pl.when(((jnp.int32(waits) >> q) & 1) == 1)
                def _():
                    arrival(step, role, m).wait_recv()

                strips.append(near.at[step, role * HALO + m])
                hs.append(role_s[role] + m)
            return strips, hs

        def near_group(q, carry):
            group(*near_strips(q))
            return carry

        lax.fori_loop(0, 8 if step == 0 else 7, near_group, 0)
        if step == 1:
            strips, hs = near_strips(jnp.int32(7))
            for k in range(4):
                multiply(strips[k], hs[k], k)
            gather(hs, None, range(1))

        total = jnp.zeros((1, 128), f32)
        for pair in range(ROWS // 2):
            total = total + trace_of(acc[pair * SLOTS], eye_both)
        traces.append(total)
        for m in range(HALO):
            out += passed_on(step, m)
        out += passed_on_last(step)
        sends += out

    row = jnp.concatenate([traces[0], traces[1], traces[1], traces[2], jnp.zeros((4, 128), f32)], axis=0)

    def exchange(value, buffer, index, count, send, recv, target):
        parts[count % 3] = value
        buffer[index] = value
        copies = []
        for k in range(1, count):
            copies.append(pltpu.make_async_remote_copy(
                src_ref=parts.at[count % 3], dst_ref=buffer.at[index], send_sem=send.at[k], recv_sem=recv.at[k],
                device_id=target(k), device_id_type=MESH))
        for copy in copies:
            copy.start()
        return copies

    def exchanged(copies, buffer, count):
        for copy in copies:
            copy.wait_recv()
        total = buffer[0]
        for k in range(1, count):
            total = total + buffer[k]
        return total

    along_y = exchange(row, sum_y, iy, ny, sumy_send, sumy_recv, lambda k: at(0, k))

    gather(hs, None, range(1, SLOTS))

    def last(pair, carry):
        for odd_row in range(2):
            g = 2 * pair + odd_row
            for q in range(4):
                tiles = []
                for half in range(2):
                    chunk = cur[1, g, :, 256 * q + 128 * half:256 * q + 128 * half + 128]
                    tiles.append(2.0 * chunk - chunk_of(pair, odd_row, 2 * q + half))
                turned = jnp.transpose(jnp.concatenate(tiles, axis=0))
                result[g, :, 256 * q:256 * q + 128] = turned[0:BLOCK]
                result[g, :, 256 * q + 128:256 * q + 256] = turned[BLOCK:]
        return carry

    lax.fori_loop(0, ROWS // 4, last, 0)
    row = exchanged(along_y, sum_y, ny)
    along_x = exchange(row, sum_x, ix, nx, sumx_send, sumx_recv, lambda k: at(k, 0))
    lax.fori_loop(ROWS // 4, ROWS // 2, last, 0)
    row = exchanged(along_x, sum_x, nx)
    scale = 1.0 / (nx * ny * ROWS * BLOCK)
    for k in range(4):
        occ_s[k] = jnp.sum(row[k:k + 1, :]) * scale

    for d in range(16):
        sends[d].wait_send()
    for copy in sends[16:] + along_y + along_x:
        copy.wait_send()


def shards(nx, ny, density, moves, cols, halo_rows):
    table = jnp.concatenate([
        cols.reshape(ROWS, SLOTS),
        jnp.pad(moves.reshape(1, ROWS), ((0, 0), (0, SLOTS - ROWS))),
        jnp.pad(halo_rows.reshape(1, HALO), ((0, 0), (0, SLOTS - HALO)))], axis=0)
    dma = pltpu.SemaphoreType.DMA
    vmem = pltpu.VMEM
    result, occupation = pl.pallas_call(
        functools.partial(kernel, nx, ny),
        out_shape=(jax.ShapeDtypeStruct((ROWS, BLOCK, STRIP), f32), jax.ShapeDtypeStruct((4,), f32)),
        in_specs=[pl.BlockSpec(memory_space=vmem), pl.BlockSpec(memory_space=pltpu.HBM)],
        out_specs=(pl.BlockSpec(memory_space=vmem), pl.BlockSpec(memory_space=pltpu.SMEM)),
        scratch_shapes=[
            pltpu.SMEM((ROWS + 2, SLOTS), i32),
            vmem((ROWS, BLOCK, STRIP), f32),
            vmem((8, BLOCK, STRIP), f32),
            vmem((8, BLOCK, STRIP), f32),
            vmem((2, ROWS, BLOCK, STRIP), f32),
            vmem((2, HALO, BLOCK, STRIP), f32),
            vmem((2, 8 * HALO, BLOCK, STRIP), f32),
            vmem((ROWS * (SLOTS + 1), 128, 128), bf16),
            vmem((4 * (SLOTS + 1), ROWS // 2, BLOCK, 128), f32),
            vmem((ROWS // 2 * SLOTS, BLOCK, 128), f32),
            vmem((16, 128), i32),
            vmem((8, 16, 128), i32),
            vmem((2 * POOL + 8, 128), i32),
            pltpu.SMEM((2 * POOL + 8, 128), i32),
            pltpu.SMEM((8,), i32),
            vmem((3, 8, 128), f32),
            vmem((ny, 8, 128), f32),
            vmem((nx, 8, 128), f32),
            dma, dma, dma,
            dma((8,)), dma((8,)), dma((8,)), dma((8,)),
            dma((2, 8 * HALO)), dma((2, 8 * HALO)),
            dma((ny,)), dma((ny,)), dma((nx,)), dma((nx,)),
        ],
        compiler_params=pltpu.CompilerParams(
            collective_id=0, has_side_effects=True, vmem_limit_bytes=50 * 1024 * 1024),
    )(table, density)
    return result.reshape(density.shape), occupation


def solution(mesh):
    nx, ny = mesh.shape["gx"], mesh.shape["gy"]
    in_specs = (
        P("gx", "gy", None, None, None),
        P("gx", "gy", None),
        P("gx", "gy", None, None),
        P("gx", "gy", None),
    )
    out_specs = (P("gx", "gy", None, None, None), P())
    return jax.shard_map(functools.partial(shards, nx, ny), mesh=mesh, in_specs=in_specs, out_specs=out_specs,
                         check_vma=False)
```

```python
import functools

import jax
import jax.numpy as jnp
from jax import lax
from jax.experimental import pallas as pl
from jax.experimental.pallas import tpu as pltpu
from jax.sharding import PartitionSpec as P

MESH = pl.DeviceIdType.MESH
f32 = jnp.float32
bf16 = jnp.bfloat16
i32 = jnp.int32

DIRS = ((-1, -1), (-1, 0), (-1, 1), (0, -1), (0, 1), (1, -1), (1, 0), (1, 1))

ROWS = 8
SLOTS = 16
BLOCK = 64
HALO = 4
STRIP = SLOTS * BLOCK
PAIRS = SLOTS // 2
POOL = ROWS + 8 * HALO

PLACE = tuple(4 * (s // 4) + (0, 2, 1, 3)[s % 4] for s in range(SLOTS))

I, Y, ZM, ZP, ZMI, ZPI, ZMY, ZPY = range(8)

ARRIVING = (
    ((I, 0), (I, 1), (I, 2), (I, 3)),
    ((Y, 3), (Y, 0), (ZM, 0), (ZP, 0)),
    ((ZMI, 0), (ZPI, 0), (Y, 1), (Y, 2)),
    ((ZM, 1), (ZP, 1), (ZMI, 1), (ZPI, 1)),
    ((ZM, 2), (ZP, 2), (ZMY, 0), (ZPY, 0)),
    ((ZMI, 2), (ZPI, 2), (ZM, 3), (ZP, 3)),
    ((ZMI, 3), (ZPI, 3), (ZMY, 1), (ZPY, 1)),
    ((ZMY, 2), (ZPY, 2), (ZMY, 3), (ZPY, 3)),
)
ARRIVING_LAST = ARRIVING[:5] + (
    ((ZMI, 2), (ZPI, 2), (ZMY, 1), (ZPY, 1)),
    ((ZP, 3), (ZPI, 3), (ZMY, 2), (ZMY, 3)),
    ((ZM, 3), (ZMI, 3), (ZPY, 2), (ZPY, 3)),
)
COUNTS = {I: 1, Y: 1, ZM: 0, ZP: 2, ZMI: 0, ZPI: 2, ZMY: 2, ZPY: 0}
PASS_BEFORE = (0, 2, 4, 5)


def kernel(nx, ny, cols, dens_hbm, result, occ_s, cols_s,
           dens, stage, mig, cur, halo, near, left, prod, acc, tsum,
           info, infos, tab, tab_s, role_s, parts, sum_y, sum_x,
           local_sem, small_sem, tab_sem, mig_send, mig_recv, info_send, info_recv,
           halo_send, halo_recv, sumy_send, sumy_recv, sumx_send, sumx_recv):
    ix = lax.axis_index("gx")
    iy = lax.axis_index("gy")
    me = ix * ny + iy
    cross = 2 * lax.rem(iy, 2) - 1
    inner = -cross

    def at(dx, dy):
        return (lax.rem(ix + dx + nx, nx), lax.rem(iy + dy + ny, ny))

    load = pltpu.make_async_copy(dens_hbm.at[0, 0], dens, local_sem)
    load.start()
    small = pltpu.make_async_copy(cols, cols_s, small_sem)
    small.start()

    barrier = pltpu.get_barrier_semaphore()
    greeted = [at(dx, dy) for dx, dy in DIRS if dx and dy]
    greeted += [at(k, 0) for k in range(1, nx)]
    greeted += [at(0, k) for k in range(1, ny)]
    for other in greeted:
        pl.semaphore_signal(barrier, inc=1, device_id=other, device_id_type=MESH)

    small.wait()

    moves = [cols_s[ROWS, r] for r in range(ROWS)]
    rims = [cols_s[ROWS + 1, m] for m in range(HALO)]
    row_for, slot_for = [], []
    for dx, dy in DIRS:
        ox, oy = at(dx, dy)
        brick = ox * ny + oy
        row, slot = jnp.int32(0), jnp.int32(-1)
        for r in range(ROWS):
            hit = (moves[r] >> 3) == brick
            row = jnp.where(hit, r, row)
            slot = jnp.where(hit, moves[r] & 7, slot)
        row_for.append(row)
        slot_for.append(slot)

    info[...] = jnp.full((16, 128), -1, i32)
    for m in range(HALO):
        info[pl.ds(m, 1), 0:SLOTS] = cols[pl.ds(rims[m], 1), :]
        info[pl.ds(HALO + m, 1), :] = jnp.full((1, 128), rims[m], i32)
    for d in range(8):
        info[pl.ds(8 + d, 1), :] = jnp.full((1, 128), slot_for[d], i32)

    for role, n in ((I, 3 + (inner + 1) // 2), (Y, 3 + (cross + 1) // 2), (ZM, 1), (ZP, 6),
                    (ZMI, inner + 1), (ZPI, inner + 6), (ZMY, cross + 1), (ZPY, cross + 6)):
        role_s[role] = jnp.int32(ROWS) + HALO * n

    def turn_row(src, dst):
        for q in range(4):
            tile = jnp.concatenate([src[:, 256 * q:256 * q + 128], src[:, 256 * q + 128:256 * q + 256]], axis=0)
            turned = jnp.transpose(tile)
            dst[:, 256 * q:256 * q + 128] = turned[0:BLOCK]
            dst[:, 256 * q + 128:256 * q + 256] = turned[BLOCK:]

    order = (1, 6, 0, 7, 2, 5, 3, 4)
    load.wait()
    for d in order[:2]:
        turn_row(dens.at[row_for[d]], stage.at[d])
    pl.semaphore_wait(barrier, len(greeted))

    sends = []
    for d, (dx, dy) in enumerate(DIRS):
        copy = pltpu.make_async_remote_copy(
            src_ref=info, dst_ref=infos.at[7 - d], send_sem=info_send.at[d], recv_sem=info_recv.at[7 - d],
            device_id=at(dx, dy), device_id_type=MESH)
        copy.start()
        sends.append(copy)
    for d in order:
        dx, dy = DIRS[d]
        if d not in order[:2]:
            turn_row(dens.at[row_for[d]], stage.at[d])
        copy = pltpu.make_async_remote_copy(
            src_ref=stage.at[d], dst_ref=mig.at[7 - d], send_sem=mig_send.at[d], recv_sem=mig_recv.at[7 - d],
            device_id=at(dx, dy), device_id_type=MESH)
        copy.start()
        sends.append(copy)

    def turn(r, carry):
        turn_row(dens.at[r], dens.at[r])
        return carry

    lax.fori_loop(0, ROWS, turn, 0)

    flat = jnp.broadcast_to(
        jnp.concatenate([cols[g:g + 1, :] for g in range(ROWS)], axis=1), (8, 128))
    slot = lax.rem(lax.broadcasted_iota(i32, (8, 128), 1), SLOTS)
    middle = lax.rem(slot, 4)
    place = slot + jnp.where(middle == 1, 1, 0) - jnp.where(middle == 2, 1, 0)
    sub = lax.broadcasted_iota(i32, (8, 128), 0)

    def matched(ids):
        found = jnp.full((8, 128), SLOTS, i32)
        for u in range(SLOTS):
            found = jnp.where(ids[:, u:u + 1] == flat, PLACE[u], found)
        return found

    tab[0:8, :] = matched(cols[0:ROWS, :])
    for group in range(POOL // 8):
        found = jnp.where(flat == sub + 8 * group, place - SLOTS, 0)
        for width in (1, 2, 4, 8):
            found = found + pltpu.roll(found, 128 - width, 1)
        found = jnp.clip(found + SLOTS, 0, SLOTS)
        tab[POOL + 8 * group:POOL + 8 * group + 8, :] = found
    for d in range(8):
        sends[d].wait_recv()
    source = jnp.zeros((8, 128), i32)
    for n in range(8):
        dx, dy = DIRS[n]
        ids = infos[n, 0:8, :]
        pos = jnp.full((8, 128), -1, i32)
        for m in range(HALO):
            pos = jnp.where(ids == infos[n, HALO + m:HALO + m + 1, :], ROWS + HALO * n + m, pos)
        for n2, (ex, ey) in enumerate(DIRS):
            there = (dx + ex, dy + ey)
            first = ROWS + HALO * n2
            if there == (0, 0):
                for m in range(HALO):
                    pos = jnp.where(ids == first + m, rims[m], pos)
            elif there in DIRS:
                shift = HALO * (DIRS.index(there) - n2)
                pos = jnp.where((ids >= first) & (ids < first + HALO), ids + shift, pos)
        tab[ROWS + HALO * n:ROWS + HALO * n + HALO, :] = matched(pos)[:HALO]
        source = jnp.where(infos[n, 8 + 7 - n:9 + 7 - n, :] == sub, n, source)
    tab[2 * POOL:2 * POOL + 8, :] = source
    to_smem = pltpu.make_async_copy(tab, tab_s, tab_sem)
    to_smem.start()

    for g in range(ROWS):
        left[g * (SLOTS + 1) + SLOTS] = jnp.zeros((128, 128), bf16)
    for k in range(4):
        prod[k * (SLOTS + 1) + SLOTS] = jnp.zeros((ROWS // 2, BLOCK, 128), f32)
    to_smem.wait()

    for d in range(8):
        sends[8 + d].wait_recv()

    def arrived(r):
        home, own = jnp.int32(0), jnp.int32(0)
        for q in range(ROWS):
            hit = moves[q] == me * ROWS + r
            home = jnp.where(hit, 1, home)
            own = jnp.where(hit, q, own)
        return jnp.where(home == 1, dens[own], mig[tab_s[2 * POOL + r, 0]])

    lanes = lax.broadcasted_iota(i32, (BLOCK, 128), 1)
    low = lanes < BLOCK
    low_wide = lax.broadcasted_iota(i32, (128, 128), 1) < BLOCK
    eye = lax.broadcasted_iota(i32, (BLOCK, 128), 0)
    eye_low = lanes == eye
    eye_both = lax.rem(lanes, BLOCK) == eye

    def trace_of(chunk, where):
        return jnp.sum(jnp.where(where, chunk, 0.0), axis=0, keepdims=True)

    def split_rows(step):
        def one(g, total):
            for q in range(PAIRS):
                chunk = cur[step, g, :, 128 * q:128 * q + 128]
                turned = pltpu.roll(chunk, BLOCK, 1)
                for odd in range(2):
                    twice = jnp.where(low, turned, chunk) if odd else jnp.where(low, chunk, turned)
                    hi = twice.astype(bf16)
                    lo = (twice - hi.astype(f32)).astype(bf16)
                    left[g * (SLOTS + 1) + 2 * q + odd, 0:BLOCK, :] = hi
                    left[g * (SLOTS + 1) + 2 * q + odd, BLOCK:128, :] = lo
            return total + trace_of(cur[step, g, :, 0:128], eye_low)

        return lax.fori_loop(0, ROWS, one, jnp.zeros((1, 128), f32))

    def multiply(strip, h, k):
        blocks = []
        for pair in range(ROWS // 2):
            even = left[2 * pair * (SLOTS + 1) + tab_s[POOL + h, SLOTS * 2 * pair]]
            odd = left[(2 * pair + 1) * (SLOTS + 1) + tab_s[POOL + h, SLOTS * (2 * pair + 1)]]
            blocks.append(jnp.where(low_wide, even, odd))
        weights = jnp.concatenate(blocks, axis=1)
        weights = jnp.concatenate([weights[0:BLOCK], weights[0:BLOCK], weights[BLOCK:], weights[BLOCK:]], axis=0)
        far = []
        for q in range(PAIRS):
            chunk = strip[:, 128 * q:128 * q + 128]
            hi = chunk.astype(bf16).astype(f32)
            lo = chunk - hi
            far.append(jnp.where(low, hi, pltpu.roll(lo, BLOCK, 1)).astype(bf16))
            far.append(jnp.where(low, pltpu.roll(hi, BLOCK, 1), lo).astype(bf16))
        far = jnp.concatenate(far, axis=0)
        far = jnp.concatenate([far, far], axis=1)
        for part in range(2):
            out = jnp.dot(far, weights[:, 256 * part:256 * part + 256], preferred_element_type=f32)
            for u in range(SLOTS):
                for half in range(2):
                    prod[k * (SLOTS + 1) + u, 2 * part + half] = out[
                        BLOCK * u:BLOCK * u + BLOCK, 128 * half:128 * half + 128]

    def gather(hs, fresh, slots=range(SLOTS)):
        def one(pair, carry):
            for s in slots:
                index = pair * SLOTS + s
                total = acc[index]
                if fresh is not None:
                    total = jnp.where(fresh, 0.0, total)
                for k in range(4):
                    even = prod[k * (SLOTS + 1) + tab_s[hs[k], 2 * SLOTS * pair + s], pair]
                    odd = prod[k * (SLOTS + 1) + tab_s[hs[k], 2 * SLOTS * pair + SLOTS + s], pair]
                    total = total + jnp.where(low, even, odd)
                acc[index] = total
            return carry

        lax.fori_loop(0, ROWS // 2, one, 0)

    def group(strips, hs, fresh=None, counts=None):
        for k in range(4):
            multiply(strips[k], hs[k], k)
        if counts is not None:
            total = tsum[...]
            for k in range(4):
                part = None
                for pair in range(ROWS // 2):
                    even = prod[k * (SLOTS + 1) + tab_s[hs[k], 2 * SLOTS * pair], pair]
                    odd = prod[k * (SLOTS + 1) + tab_s[hs[k], 2 * SLOTS * pair + SLOTS], pair]
                    block = jnp.where(low, even, odd)
                    part = block if part is None else part + block
                total = total + counts[k] * part
            tsum[...] = total
        gather(hs, fresh)

    def halo_copy(step, src, role, m, target):
        place = role * HALO + m
        return pltpu.make_async_remote_copy(
            src_ref=src, dst_ref=near.at[step, place], send_sem=halo_send.at[step, place],
            recv_sem=halo_recv.at[step, place], device_id=target, device_id_type=MESH)

    def arrival(step, role, m):
        return halo_copy(step, near.at[step, role * HALO + m], role, m, at(0, 1))

    def passed_on(step, m, roles=(ZM, ZP)):
        out = []
        for role, inside, outside in ((ZM, ZMI, ZMY), (ZP, ZPI, ZPY)):
            if role not in roles:
                continue
            src = near.at[step, role * HALO + m]
            if m < HALO - 1:
                out.append(halo_copy(step, src, outside, m, at(0, cross)))
            out.append(halo_copy(step, src, inside, m, at(0, inner)))
        return out

    def passed_on_last(step):
        src = near.at[step, Y * HALO + HALO - 1]
        return [halo_copy(step, src, ZPY, HALO - 1, at(-1, 0)), halo_copy(step, src, ZMY, HALO - 1, at(1, 0))]

    def pass_on(step, m, roles=(ZM, ZP)):
        for role in roles:
            arrival(step, role, m).wait_recv()
        for copy in passed_on(step, m, roles):
            copy.start()

    def pass_on_last(step):
        arrival(step, Y, HALO - 1).wait_recv()
        for copy in passed_on_last(step):
            copy.start()
        if step == 1:
            last_along_x(step).start()

    def last_along_x(step):
        return halo_copy(step, halo.at[step, HALO - 1], ZM, HALO - 1, at(1, 0))

    def chunk_of(pair, odd, q):
        first = acc[pair * SLOTS + PLACE[2 * q]]
        second = acc[pair * SLOTS + PLACE[2 * q + 1]]
        if odd:
            return jnp.where(low, pltpu.roll(first, BLOCK, 1), second)
        return jnp.where(low, first, pltpu.roll(second, BLOCK, 1))

    def combine(row, q):
        return jnp.where((row & 1) == 1, chunk_of(row >> 1, True, q), chunk_of(row >> 1, False, q))

    traces = []
    for step in range(2):
        out = []

        def send(role, m, target):
            out.append(halo_copy(step, halo.at[step, m], role, m, target))
            out[-1].start()

        for m in (3, 0, 1, 2):
            if step == 0:
                halo[step, m] = arrived(rims[m])
            else:
                for q in range(PAIRS):
                    halo[step, m, :, 128 * q:128 * q + 128] = combine(rims[m], q)
            send(Y, m, at(0, cross))
            if m < 3:
                send(ZP, m, at(-1, 0))
                send(ZM, m, at(1, 0))
        send(ZP, 3, at(-1, 0))
        if step == 0:
            send(ZM, 3, at(1, 0))
        for m in range(HALO):
            send(I, m, at(0, inner))

        def settle(r, carry):
            if step == 0:
                cur[0, r] = arrived(r)
            else:
                for odd in range(2):
                    for q in range(PAIRS):
                        cur[1, 2 * r + odd, :, 128 * q:128 * q + 128] = chunk_of(r, odd, q)
            return carry

        lax.fori_loop(0, ROWS if step == 0 else ROWS // 2, settle, 0)
        before = split_rows(step)
        if step == 0:
            traces.append(before)

        def own_group(i, carry):
            group([cur.at[step, 4 * i + k] for k in range(4)], [4 * i + k for k in range(4)], i == 0,
                  [1.0] * 4 if step == 1 else None)
            return carry

        if step == 1:
            tsum[...] = jnp.zeros((BLOCK, 128), f32)
        lax.fori_loop(0, 2, own_group, 0)

        def near_strips(q):
            for m in range(HALO):
                if step == 1 and m == HALO - 1:
                    for before, role in ((6, ZP), (7, ZM)):
                        @pl.when(q == before)
                        def _():
                            pass_on(step, m, (role,))

                    continue

                @pl.when(q == PASS_BEFORE[m])
                def _():
                    pass_on(step, m)
                    if m == 0:
                        pass_on_last(step)

            order_of = (ARRIVING, ARRIVING_LAST)[step]
            strips, hs, counts = [], [], []
            for k in range(4):
                roles = sum(four[k][0] << (3 * j) for j, four in enumerate(order_of))
                rows = sum(four[k][1] << (2 * j) for j, four in enumerate(order_of))
                waits = sum(int(not (four[k][0] in (ZM, ZP) or four[k] == (Y, 3))) << j for j, four in enumerate(order_of))
                role = (jnp.int32(roles) >> (3 * q)) & 7
                m = (jnp.int32(rows) >> (2 * q)) & 3

                @pl.when(((jnp.int32(waits) >> q) & 1) == 1)
                def _():
                    arrival(step, role, m).wait_recv()

                strips.append(near.at[step, role * HALO + m])
                hs.append(role_s[role] + m)
                twice = sum(count << (2 * role_) for role_, count in COUNTS.items())
                counts.append(((jnp.int32(twice) >> (2 * role)) & 3).astype(f32))
            return strips, hs, None, counts if step == 1 else None

        def near_group(q, carry):
            group(*near_strips(q))
            return carry

        lax.fori_loop(0, 8 if step == 0 else 7, near_group, 0)
        total = tsum[...] if step == 1 else sum(acc[pair * SLOTS] for pair in range(ROWS // 2))
        traces.append(trace_of(total, eye_both))
        for m in range(HALO):
            out += passed_on(step, m)
        out += passed_on_last(step)
        if step == 1:
            out.append(last_along_x(step))
        sends += out

    row = jnp.concatenate([traces[0], traces[1], traces[1], traces[2], jnp.zeros((4, 128), f32)], axis=0)

    def exchange(value, buffer, index, count, send, recv, target):
        parts[count % 3] = value
        buffer[index] = value
        copies = []
        for k in range(1, count):
            copies.append(pltpu.make_async_remote_copy(
                src_ref=parts.at[count % 3], dst_ref=buffer.at[index], send_sem=send.at[k], recv_sem=recv.at[k],
                device_id=target(k), device_id_type=MESH))
        for copy in copies:
            copy.start()
        return copies

    def exchanged(copies, buffer, count):
        for copy in copies:
            copy.wait_recv()
        total = buffer[0]
        for k in range(1, count):
            total = total + buffer[k]
        return total

    along_y = exchange(row, sum_y, iy, ny, sumy_send, sumy_recv, lambda k: at(0, k))

    group(*near_strips(jnp.int32(7))[:2])

    def last(pair, carry):
        for odd_row in range(2):
            g = 2 * pair + odd_row
            for q in range(4):
                tiles = []
                for half in range(2):
                    chunk = cur[1, g, :, 256 * q + 128 * half:256 * q + 128 * half + 128]
                    tiles.append(2.0 * chunk - chunk_of(pair, odd_row, 2 * q + half))
                turned = jnp.transpose(jnp.concatenate(tiles, axis=0))
                result[g, :, 256 * q:256 * q + 128] = turned[0:BLOCK]
                result[g, :, 256 * q + 128:256 * q + 256] = turned[BLOCK:]
        return carry

    row = exchanged(along_y, sum_y, ny)
    along_x = exchange(row, sum_x, ix, nx, sumx_send, sumx_recv, lambda k: at(k, 0))
    lax.fori_loop(0, ROWS // 2, last, 0)
    row = exchanged(along_x, sum_x, nx)
    scale = 1.0 / (nx * ny * ROWS * BLOCK)
    for k in range(4):
        occ_s[k] = jnp.sum(row[k:k + 1, :]) * scale

    for d in range(16):
        sends[d].wait_send()
    for copy in sends[16:] + along_y + along_x:
        copy.wait_send()


def shards(nx, ny, density, moves, cols, halo_rows):
    table = jnp.concatenate([
        cols.reshape(ROWS, SLOTS),
        jnp.pad(moves.reshape(1, ROWS), ((0, 0), (0, SLOTS - ROWS))),
        jnp.pad(halo_rows.reshape(1, HALO), ((0, 0), (0, SLOTS - HALO)))], axis=0)
    dma = pltpu.SemaphoreType.DMA
    vmem = pltpu.VMEM
    result, occupation = pl.pallas_call(
        functools.partial(kernel, nx, ny),
        out_shape=(jax.ShapeDtypeStruct((ROWS, BLOCK, STRIP), f32), jax.ShapeDtypeStruct((4,), f32)),
        in_specs=[pl.BlockSpec(memory_space=vmem), pl.BlockSpec(memory_space=pltpu.HBM)],
        out_specs=(pl.BlockSpec(memory_space=vmem), pl.BlockSpec(memory_space=pltpu.SMEM)),
        scratch_shapes=[
            pltpu.SMEM((ROWS + 2, SLOTS), i32),
            vmem((ROWS, BLOCK, STRIP), f32),
            vmem((8, BLOCK, STRIP), f32),
            vmem((8, BLOCK, STRIP), f32),
            vmem((2, ROWS, BLOCK, STRIP), f32),
            vmem((2, HALO, BLOCK, STRIP), f32),
            vmem((2, 8 * HALO, BLOCK, STRIP), f32),
            vmem((ROWS * (SLOTS + 1), 128, 128), bf16),
            vmem((4 * (SLOTS + 1), ROWS // 2, BLOCK, 128), f32),
            vmem((ROWS // 2 * SLOTS, BLOCK, 128), f32),
            vmem((BLOCK, 128), f32),
            vmem((16, 128), i32),
            vmem((8, 16, 128), i32),
            vmem((2 * POOL + 8, 128), i32),
            pltpu.SMEM((2 * POOL + 8, 128), i32),
            pltpu.SMEM((8,), i32),
            vmem((3, 8, 128), f32),
            vmem((ny, 8, 128), f32),
            vmem((nx, 8, 128), f32),
            dma, dma, dma,
            dma((8,)), dma((8,)), dma((8,)), dma((8,)),
            dma((2, 8 * HALO)), dma((2, 8 * HALO)),
            dma((ny,)), dma((ny,)), dma((nx,)), dma((nx,)),
        ],
        compiler_params=pltpu.CompilerParams(
            collective_id=0, has_side_effects=True, vmem_limit_bytes=50 * 1024 * 1024),
    )(table, density)
    return result.reshape(density.shape), occupation


def solution(mesh):
    nx, ny = mesh.shape["gx"], mesh.shape["gy"]
    in_specs = (
        P("gx", "gy", None, None, None),
        P("gx", "gy", None),
        P("gx", "gy", None, None),
        P("gx", "gy", None),
    )
    out_specs = (P("gx", "gy", None, None, None), P())
    return jax.shard_map(functools.partial(shards, nx, ny), mesh=mesh, in_specs=in_specs, out_specs=out_specs,
                         check_vma=False)
```

```python
import functools

import jax
import jax.numpy as jnp
from jax import lax
from jax.experimental import pallas as pl
from jax.experimental.pallas import tpu as pltpu
from jax.sharding import PartitionSpec as P

MESH = pl.DeviceIdType.MESH
f32 = jnp.float32
bf16 = jnp.bfloat16
i32 = jnp.int32

DIRS = ((-1, -1), (-1, 0), (-1, 1), (0, -1), (0, 1), (1, -1), (1, 0), (1, 1))

ROWS = 8
SLOTS = 16
BLOCK = 64
HALO = 4
STRIP = SLOTS * BLOCK
PAIRS = SLOTS // 2
POOL = ROWS + 8 * HALO

PLACE = tuple(4 * (s // 4) + (0, 2, 1, 3)[s % 4] for s in range(SLOTS))

I, Y, ZM, ZP, ZMI, ZPI, ZMY, ZPY = range(8)

ARRIVING = (
    ((I, 0), (I, 1), (I, 2), (I, 3)),
    ((Y, 3), (Y, 0), (ZM, 0), (ZP, 0)),
    ((ZMI, 0), (ZPI, 0), (Y, 1), (Y, 2)),
    ((ZM, 1), (ZP, 1), (ZMI, 1), (ZPI, 1)),
    ((ZM, 2), (ZP, 2), (ZMY, 0), (ZPY, 0)),
    ((ZMI, 2), (ZPI, 2), (ZM, 3), (ZP, 3)),
    ((ZMI, 3), (ZPI, 3), (ZMY, 1), (ZPY, 1)),
    ((ZMY, 2), (ZPY, 2), (ZMY, 3), (ZPY, 3)),
)
ARRIVING_LAST = ARRIVING[:5] + (
    ((ZMI, 2), (ZPI, 2), (ZMY, 1), (ZPY, 1)),
    ((ZP, 3), (ZPI, 3), (ZMY, 2), (ZMY, 3)),
    ((ZM, 3), (ZMI, 3), (ZPY, 2), (ZPY, 3)),
)
COUNTS = {I: 1, Y: 1, ZM: 0, ZP: 2, ZMI: 0, ZPI: 2, ZMY: 2, ZPY: 0}
PASS_BEFORE = (0, 2, 4, 5)


def kernel(nx, ny, cols, dens_hbm, result, occ_s, cols_s,
           dens, stage, mig, cur, halo, near, left, prod, acc, tsum,
           info, infos, tab, tab_s, role_s, parts, sum_y, sum_x,
           local_sem, small_sem, tab_sem, mig_send, mig_recv, info_send, info_recv,
           halo_send, halo_recv, sumy_send, sumy_recv, sumx_send, sumx_recv):
    ix = lax.axis_index("gx")
    iy = lax.axis_index("gy")
    me = ix * ny + iy
    cross = 2 * lax.rem(iy, 2) - 1
    inner = -cross

    def at(dx, dy):
        return (lax.rem(ix + dx + nx, nx), lax.rem(iy + dy + ny, ny))

    load = pltpu.make_async_copy(dens_hbm.at[0, 0], dens, local_sem)
    load.start()
    small = pltpu.make_async_copy(cols, cols_s, small_sem)
    small.start()

    barrier = pltpu.get_barrier_semaphore()
    greeted = [at(dx, dy) for dx, dy in DIRS if dx and dy]
    greeted += [at(k, 0) for k in range(1, nx)]
    greeted += [at(0, k) for k in range(1, ny)]
    for other in greeted:
        pl.semaphore_signal(barrier, inc=1, device_id=other, device_id_type=MESH)

    small.wait()

    moves = [cols_s[ROWS, r] for r in range(ROWS)]
    rims = [cols_s[ROWS + 1, m] for m in range(HALO)]
    row_for, slot_for = [], []
    for dx, dy in DIRS:
        ox, oy = at(dx, dy)
        brick = ox * ny + oy
        row, slot = jnp.int32(0), jnp.int32(-1)
        for r in range(ROWS):
            hit = (moves[r] >> 3) == brick
            row = jnp.where(hit, r, row)
            slot = jnp.where(hit, moves[r] & 7, slot)
        row_for.append(row)
        slot_for.append(slot)

    info[...] = jnp.full((16, 128), -1, i32)
    for m in range(HALO):
        info[pl.ds(m, 1), 0:SLOTS] = cols[pl.ds(rims[m], 1), :]
        info[pl.ds(HALO + m, 1), :] = jnp.full((1, 128), rims[m], i32)
    for d in range(8):
        info[pl.ds(8 + d, 1), :] = jnp.full((1, 128), slot_for[d], i32)

    for role, n in ((I, 3 + (inner + 1) // 2), (Y, 3 + (cross + 1) // 2), (ZM, 1), (ZP, 6),
                    (ZMI, inner + 1), (ZPI, inner + 6), (ZMY, cross + 1), (ZPY, cross + 6)):
        role_s[role] = jnp.int32(ROWS) + HALO * n

    def turn_row(src, dst):
        for q in range(4):
            tile = jnp.concatenate([src[:, 256 * q:256 * q + 128], src[:, 256 * q + 128:256 * q + 256]], axis=0)
            turned = jnp.transpose(tile)
            dst[:, 256 * q:256 * q + 128] = turned[0:BLOCK]
            dst[:, 256 * q + 128:256 * q + 256] = turned[BLOCK:]

    order = (1, 6, 0, 7, 2, 5, 3, 4)
    load.wait()
    for d in order[:2]:
        turn_row(dens.at[row_for[d]], stage.at[d])
    pl.semaphore_wait(barrier, len(greeted))

    sends = []
    for d, (dx, dy) in enumerate(DIRS):
        copy = pltpu.make_async_remote_copy(
            src_ref=info, dst_ref=infos.at[7 - d], send_sem=info_send.at[d], recv_sem=info_recv.at[7 - d],
            device_id=at(dx, dy), device_id_type=MESH)
        copy.start()
        sends.append(copy)
    for d in order:
        dx, dy = DIRS[d]
        if d not in order[:2]:
            turn_row(dens.at[row_for[d]], stage.at[d])
        copy = pltpu.make_async_remote_copy(
            src_ref=stage.at[d], dst_ref=mig.at[7 - d], send_sem=mig_send.at[d], recv_sem=mig_recv.at[7 - d],
            device_id=at(dx, dy), device_id_type=MESH)
        copy.start()
        sends.append(copy)

    def turn(r, carry):
        turn_row(dens.at[r], dens.at[r])
        return carry

    lax.fori_loop(0, ROWS, turn, 0)

    flat = jnp.broadcast_to(
        jnp.concatenate([cols[g:g + 1, :] for g in range(ROWS)], axis=1), (8, 128))
    slot = lax.rem(lax.broadcasted_iota(i32, (8, 128), 1), SLOTS)
    middle = lax.rem(slot, 4)
    place = slot + jnp.where(middle == 1, 1, 0) - jnp.where(middle == 2, 1, 0)
    sub = lax.broadcasted_iota(i32, (8, 128), 0)

    def matched(ids):
        found = jnp.full((8, 128), SLOTS, i32)
        for u in range(SLOTS):
            found = jnp.where(ids[:, u:u + 1] == flat, PLACE[u], found)
        return found

    tab[0:8, :] = matched(cols[0:ROWS, :])
    for group in range(POOL // 8):
        found = jnp.where(flat == sub + 8 * group, place - SLOTS, 0)
        for width in (1, 2, 4, 8):
            found = found + pltpu.roll(found, 128 - width, 1)
        found = jnp.clip(found + SLOTS, 0, SLOTS)
        tab[POOL + 8 * group:POOL + 8 * group + 8, :] = found
    for d in range(8):
        sends[d].wait_recv()
    source = jnp.zeros((8, 128), i32)
    for n in range(8):
        dx, dy = DIRS[n]
        ids = infos[n, 0:8, :]
        pos = jnp.full((8, 128), -1, i32)
        for m in range(HALO):
            pos = jnp.where(ids == infos[n, HALO + m:HALO + m + 1, :], ROWS + HALO * n + m, pos)
        for n2, (ex, ey) in enumerate(DIRS):
            there = (dx + ex, dy + ey)
            first = ROWS + HALO * n2
            if there == (0, 0):
                for m in range(HALO):
                    pos = jnp.where(ids == first + m, rims[m], pos)
            elif there in DIRS:
                shift = HALO * (DIRS.index(there) - n2)
                pos = jnp.where((ids >= first) & (ids < first + HALO), ids + shift, pos)
        tab[ROWS + HALO * n:ROWS + HALO * n + HALO, :] = matched(pos)[:HALO]
        source = jnp.where(infos[n, 8 + 7 - n:9 + 7 - n, :] == sub, n, source)
    tab[2 * POOL:2 * POOL + 8, :] = source
    to_smem = pltpu.make_async_copy(tab, tab_s, tab_sem)
    to_smem.start()

    for g in range(ROWS):
        left[g * (SLOTS + 1) + SLOTS] = jnp.zeros((128, 128), bf16)
    for k in range(4):
        prod[k * (SLOTS + 1) + SLOTS] = jnp.zeros((ROWS // 2, BLOCK, 128), f32)
    to_smem.wait()

    for d in range(8):
        sends[8 + d].wait_recv()

    def arrived(r):
        home, own = jnp.int32(0), jnp.int32(0)
        for q in range(ROWS):
            hit = moves[q] == me * ROWS + r
            home = jnp.where(hit, 1, home)
            own = jnp.where(hit, q, own)
        return jnp.where(home == 1, dens[own], mig[tab_s[2 * POOL + r, 0]])

    lanes = lax.broadcasted_iota(i32, (BLOCK, 128), 1)
    low = lanes < BLOCK
    low_wide = lax.broadcasted_iota(i32, (128, 128), 1) < BLOCK
    eye = lax.broadcasted_iota(i32, (BLOCK, 128), 0)
    eye_low = lanes == eye
    eye_both = lax.rem(lanes, BLOCK) == eye

    def trace_of(chunk, where):
        return jnp.sum(jnp.where(where, chunk, 0.0), axis=0, keepdims=True)

    def split_rows(step):
        def one(g, total):
            for q in range(PAIRS):
                chunk = cur[step, g, :, 128 * q:128 * q + 128]
                turned = pltpu.roll(chunk, BLOCK, 1)
                for odd in range(2):
                    twice = jnp.where(low, turned, chunk) if odd else jnp.where(low, chunk, turned)
                    hi = twice.astype(bf16)
                    lo = (twice - hi.astype(f32)).astype(bf16)
                    left[g * (SLOTS + 1) + 2 * q + odd, 0:BLOCK, :] = hi
                    left[g * (SLOTS + 1) + 2 * q + odd, BLOCK:128, :] = lo
            return total + trace_of(cur[step, g, :, 0:128], eye_low)

        return lax.fori_loop(0, ROWS, one, jnp.zeros((1, 128), f32))

    def multiply(strip, h, k):
        blocks = []
        for pair in range(ROWS // 2):
            even = left[2 * pair * (SLOTS + 1) + tab_s[POOL + h, SLOTS * 2 * pair]]
            odd = left[(2 * pair + 1) * (SLOTS + 1) + tab_s[POOL + h, SLOTS * (2 * pair + 1)]]
            blocks.append(jnp.where(low_wide, even, odd))
        weights = jnp.concatenate(blocks, axis=1)
        weights = jnp.concatenate([weights[0:BLOCK], weights[0:BLOCK], weights[BLOCK:], weights[BLOCK:]], axis=0)
        far = []
        for q in range(PAIRS):
            chunk = strip[:, 128 * q:128 * q + 128]
            hi = chunk.astype(bf16).astype(f32)
            lo = chunk - hi
            far.append(jnp.where(low, hi, pltpu.roll(lo, BLOCK, 1)).astype(bf16))
            far.append(jnp.where(low, pltpu.roll(hi, BLOCK, 1), lo).astype(bf16))
        far = jnp.concatenate(far, axis=0)
        far = jnp.concatenate([far, far], axis=1)
        for part in range(2):
            out = jnp.dot(far, weights[:, 256 * part:256 * part + 256], preferred_element_type=f32)
            for u in range(SLOTS):
                for half in range(2):
                    prod[k * (SLOTS + 1) + u, 2 * part + half] = out[
                        BLOCK * u:BLOCK * u + BLOCK, 128 * half:128 * half + 128]

    def gather(hs, fresh, slots=range(SLOTS)):
        def one(pair, carry):
            for s in slots:
                index = pair * SLOTS + s
                total = acc[index]
                if fresh is not None:
                    total = jnp.where(fresh, 0.0, total)
                for k in range(4):
                    even = prod[k * (SLOTS + 1) + tab_s[hs[k], 2 * SLOTS * pair + s], pair]
                    odd = prod[k * (SLOTS + 1) + tab_s[hs[k], 2 * SLOTS * pair + SLOTS + s], pair]
                    total = total + jnp.where(low, even, odd)
                acc[index] = total
            return carry

        lax.fori_loop(0, ROWS // 2, one, 0)

    def group(strips, hs, fresh=None, counts=None):
        for k in range(4):
            multiply(strips[k], hs[k], k)
        if counts is not None:
            total = tsum[...]
            for k in range(4):
                part = None
                for pair in range(ROWS // 2):
                    even = prod[k * (SLOTS + 1) + tab_s[hs[k], 2 * SLOTS * pair], pair]
                    odd = prod[k * (SLOTS + 1) + tab_s[hs[k], 2 * SLOTS * pair + SLOTS], pair]
                    block = jnp.where(low, even, odd)
                    part = block if part is None else part + block
                total = total + counts[k] * part
            tsum[...] = total
        gather(hs, fresh)

    def halo_copy(step, src, role, m, target):
        place = role * HALO + m
        return pltpu.make_async_remote_copy(
            src_ref=src, dst_ref=near.at[step, place], send_sem=halo_send.at[step, place],
            recv_sem=halo_recv.at[step, place], device_id=target, device_id_type=MESH)

    def arrival(step, role, m):
        return halo_copy(step, near.at[step, role * HALO + m], role, m, at(0, 1))

    def passed_on(step, m, roles=(ZM, ZP)):
        out = []
        for role, inside, outside in ((ZM, ZMI, ZMY), (ZP, ZPI, ZPY)):
            if role not in roles:
                continue
            src = near.at[step, role * HALO + m]
            if m < HALO - 1:
                out.append(halo_copy(step, src, outside, m, at(0, cross)))
            out.append(halo_copy(step, src, inside, m, at(0, inner)))
        return out

    def passed_on_last(step):
        src = near.at[step, Y * HALO + HALO - 1]
        return [halo_copy(step, src, ZPY, HALO - 1, at(-1, 0)), halo_copy(step, src, ZMY, HALO - 1, at(1, 0))]

    def pass_on(step, m, roles=(ZM, ZP)):
        for role in roles:
            arrival(step, role, m).wait_recv()
        for copy in passed_on(step, m, roles):
            copy.start()

    def pass_on_last(step):
        arrival(step, Y, HALO - 1).wait_recv()
        for copy in passed_on_last(step):
            copy.start()
        if step == 1:
            last_along_x(step).start()

    def last_along_x(step):
        return halo_copy(step, halo.at[step, HALO - 1], ZM, HALO - 1, at(1, 0))

    def chunk_of(pair, odd, q):
        first = acc[pair * SLOTS + PLACE[2 * q]]
        second = acc[pair * SLOTS + PLACE[2 * q + 1]]
        if odd:
            return jnp.where(low, pltpu.roll(first, BLOCK, 1), second)
        return jnp.where(low, first, pltpu.roll(second, BLOCK, 1))

    def combine(row, q):
        return jnp.where((row & 1) == 1, chunk_of(row >> 1, True, q), chunk_of(row >> 1, False, q))

    traces = []
    for step in range(2):
        out = []

        def send(role, m, target):
            out.append(halo_copy(step, halo.at[step, m], role, m, target))
            out[-1].start()

        for m in (3, 0, 1, 2):
            if step == 0:
                halo[step, m] = arrived(rims[m])
            else:
                for q in range(PAIRS):
                    halo[step, m, :, 128 * q:128 * q + 128] = combine(rims[m], q)
            send(Y, m, at(0, cross))
            if m < 3:
                send(ZP, m, at(-1, 0))
                send(ZM, m, at(1, 0))
        send(ZP, 3, at(-1, 0))
        if step == 0:
            send(ZM, 3, at(1, 0))
        for m in range(HALO):
            send(I, m, at(0, inner))

        def settle(r, carry):
            if step == 0:
                cur[0, r] = arrived(r)
            else:
                for odd in range(2):
                    for q in range(PAIRS):
                        cur[1, 2 * r + odd, :, 128 * q:128 * q + 128] = chunk_of(r, odd, q)
            return carry

        lax.fori_loop(0, ROWS if step == 0 else ROWS // 2, settle, 0)
        before = split_rows(step)
        if step == 0:
            traces.append(before)

        def own_group(i, carry):
            group([cur.at[step, 4 * i + k] for k in range(4)], [4 * i + k for k in range(4)], i == 0,
                  [1.0] * 4 if step == 1 else None)
            return carry

        if step == 1:
            tsum[...] = jnp.zeros((BLOCK, 128), f32)
        lax.fori_loop(0, 2, own_group, 0)

        def near_strips(q):
            for m in range(HALO):
                if step == 1 and m == HALO - 1:
                    for before, role in ((6, ZP), (7, ZM)):
                        @pl.when(q == before)
                        def _():
                            pass_on(step, m, (role,))

                    continue

                @pl.when(q == PASS_BEFORE[m])
                def _():
                    pass_on(step, m)
                    if m == 0:
                        pass_on_last(step)

            order_of = (ARRIVING, ARRIVING_LAST)[step]
            strips, hs, counts = [], [], []
            for k in range(4):
                roles = sum(four[k][0] << (3 * j) for j, four in enumerate(order_of))
                rows = sum(four[k][1] << (2 * j) for j, four in enumerate(order_of))
                waits = sum(int(not (four[k][0] in (ZM, ZP) or four[k] == (Y, 3))) << j for j, four in enumerate(order_of))
                role = (jnp.int32(roles) >> (3 * q)) & 7
                m = (jnp.int32(rows) >> (2 * q)) & 3

                @pl.when(((jnp.int32(waits) >> q) & 1) == 1)
                def _():
                    arrival(step, role, m).wait_recv()

                strips.append(near.at[step, role * HALO + m])
                hs.append(role_s[role] + m)
                twice = sum(count << (2 * role_) for role_, count in COUNTS.items())
                counts.append(((jnp.int32(twice) >> (2 * role)) & 3).astype(f32))
            return strips, hs, None, counts if step == 1 else None

        def near_group(q, carry):
            group(*near_strips(q))
            return carry

        lax.fori_loop(0, 8 if step == 0 else 7, near_group, 0)
        total = tsum[...] if step == 1 else sum(acc[pair * SLOTS] for pair in range(ROWS // 2))
        traces.append(trace_of(total, eye_both))
        for m in range(HALO):
            out += passed_on(step, m)
        out += passed_on_last(step)
        if step == 1:
            out.append(last_along_x(step))
        sends += out

    row = jnp.concatenate([traces[0], traces[1], traces[1], traces[2], jnp.zeros((4, 128), f32)], axis=0)

    def exchange(value, buffer, index, count, send, recv, target):
        parts[count % 3] = value
        buffer[index] = value
        copies = []
        for k in range(1, count):
            copies.append(pltpu.make_async_remote_copy(
                src_ref=parts.at[count % 3], dst_ref=buffer.at[index], send_sem=send.at[k], recv_sem=recv.at[k],
                device_id=target(k), device_id_type=MESH))
        for copy in copies:
            copy.start()
        return copies

    def exchanged(copies, buffer, count):
        for copy in copies:
            copy.wait_recv()
        total = buffer[0]
        for k in range(1, count):
            total = total + buffer[k]
        return total

    along_y = exchange(row, sum_y, iy, ny, sumy_send, sumy_recv, lambda k: at(0, k))

    strips, hs = near_strips(jnp.int32(7))[:2]
    for k in range(4):
        multiply(strips[k], hs[k], k)
    row = exchanged(along_y, sum_y, ny)
    along_x = exchange(row, sum_x, ix, nx, sumx_send, sumx_recv, lambda k: at(k, 0))
    gather(hs, None)

    def last(pair, carry):
        for odd_row in range(2):
            g = 2 * pair + odd_row
            for q in range(4):
                tiles = []
                for half in range(2):
                    chunk = cur[1, g, :, 256 * q + 128 * half:256 * q + 128 * half + 128]
                    tiles.append(2.0 * chunk - chunk_of(pair, odd_row, 2 * q + half))
                turned = jnp.transpose(jnp.concatenate(tiles, axis=0))
                result[g, :, 256 * q:256 * q + 128] = turned[0:BLOCK]
                result[g, :, 256 * q + 128:256 * q + 256] = turned[BLOCK:]
        return carry

    lax.fori_loop(0, ROWS // 2, last, 0)
    row = exchanged(along_x, sum_x, nx)
    scale = 1.0 / (nx * ny * ROWS * BLOCK)
    for k in range(4):
        occ_s[k] = jnp.sum(row[k:k + 1, :]) * scale

    for d in range(16):
        sends[d].wait_send()
    for copy in sends[16:] + along_y + along_x:
        copy.wait_send()


def shards(nx, ny, density, moves, cols, halo_rows):
    table = jnp.concatenate([
        cols.reshape(ROWS, SLOTS),
        jnp.pad(moves.reshape(1, ROWS), ((0, 0), (0, SLOTS - ROWS))),
        jnp.pad(halo_rows.reshape(1, HALO), ((0, 0), (0, SLOTS - HALO)))], axis=0)
    dma = pltpu.SemaphoreType.DMA
    vmem = pltpu.VMEM
    result, occupation = pl.pallas_call(
        functools.partial(kernel, nx, ny),
        out_shape=(jax.ShapeDtypeStruct((ROWS, BLOCK, STRIP), f32), jax.ShapeDtypeStruct((4,), f32)),
        in_specs=[pl.BlockSpec(memory_space=vmem), pl.BlockSpec(memory_space=pltpu.HBM)],
        out_specs=(pl.BlockSpec(memory_space=vmem), pl.BlockSpec(memory_space=pltpu.SMEM)),
        scratch_shapes=[
            pltpu.SMEM((ROWS + 2, SLOTS), i32),
            vmem((ROWS, BLOCK, STRIP), f32),
            vmem((8, BLOCK, STRIP), f32),
            vmem((8, BLOCK, STRIP), f32),
            vmem((2, ROWS, BLOCK, STRIP), f32),
            vmem((2, HALO, BLOCK, STRIP), f32),
            vmem((2, 8 * HALO, BLOCK, STRIP), f32),
            vmem((ROWS * (SLOTS + 1), 128, 128), bf16),
            vmem((4 * (SLOTS + 1), ROWS // 2, BLOCK, 128), f32),
            vmem((ROWS // 2 * SLOTS, BLOCK, 128), f32),
            vmem((BLOCK, 128), f32),
            vmem((16, 128), i32),
            vmem((8, 16, 128), i32),
            vmem((2 * POOL + 8, 128), i32),
            pltpu.SMEM((2 * POOL + 8, 128), i32),
            pltpu.SMEM((8,), i32),
            vmem((3, 8, 128), f32),
            vmem((ny, 8, 128), f32),
            vmem((nx, 8, 128), f32),
            dma, dma, dma,
            dma((8,)), dma((8,)), dma((8,)), dma((8,)),
            dma((2, 8 * HALO)), dma((2, 8 * HALO)),
            dma((ny,)), dma((ny,)), dma((nx,)), dma((nx,)),
        ],
        compiler_params=pltpu.CompilerParams(
            collective_id=0, has_side_effects=True, vmem_limit_bytes=50 * 1024 * 1024),
    )(table, density)
    return result.reshape(density.shape), occupation


def solution(mesh):
    nx, ny = mesh.shape["gx"], mesh.shape["gy"]
    in_specs = (
        P("gx", "gy", None, None, None),
        P("gx", "gy", None),
        P("gx", "gy", None, None),
        P("gx", "gy", None),
    )
    out_specs = (P("gx", "gy", None, None, None), P())
    return jax.shard_map(functools.partial(shards, nx, ny), mesh=mesh, in_specs=in_specs, out_specs=out_specs,
                         check_vma=False)
```
